512 devices in a mesh: dp: 8 (over x, core), ctx: 64 (over z, y).
Axes of the slice: x: 4, y: 8, z: 8, core: 2. Of those that a mesh axis runs over, the one named last changes fastest.
Arguments:
- queries: bfloat16 [8, 32768, 256], P('dp', 'ctx'), may hold values from -6 to 6
- keys: bfloat16 [8, 32768, 256], P('dp', 'ctx'), may hold values from -6 to 6
- values: bfloat16 [8, 32768, 256], P('dp', 'ctx'), may hold values from -6 to 6
- out_grad: bfloat16 [8, 32768, 256], P('dp', 'ctx'), may hold values from -6 to 6
- q_gain: float32 [256], replicated, may hold values from 0.25 to 1.75
- offsets: int32 [8, 64], P('dp', 'ctx'), may hold values from 0 to 131071
Outputs:
- grad_queries: bfloat16 [8, 32768, 256], P('dp', 'ctx')
- grad_keys: bfloat16 [8, 32768, 256], P('dp', 'ctx')
- grad_values: bfloat16 [8, 32768, 256], P('dp', 'ctx')
- grad_gain: float32 [256], replicated
The draws below stay inside these ranges and needn't reach their ends.
All inputs are finite; a program needn't handle non-finite values.
Results may differ from the reference program's by a relative error of at most 0.011.
Values sent between devices are 32-bit elements; how exact they have to be, the bound alone decides.
No kernel may reach another device: no remote copies, remote signals or barrier semaphores. Data moves between devices by JAX's collectives and lax.ppermute only.
A program may use at most 128 MiB of HBM per device.

```python
import jax
import jax.numpy as jnp
from jax import lax

HEADS = 2
HEAD_DIM = 128
BLOCK = 512
TOK_DEV = 512
SEQLEN = 32768
SEQS = 8
N_CTX = 64


def touch_ends(drawn, stream_key, least, largest):
    longest = drawn.shape.index(max(drawn.shape))
    spots = []
    for shift in (0, 1):
        where = [jax.random.randint(jax.random.fold_in(stream_key, axis), (), 0, length) for axis, length in enumerate(drawn.shape)]
        where[longest] = (where[longest] + shift) % drawn.shape[longest]
        spots.append(tuple(where))
    return drawn.at[spots[0]].set(least).at[spots[1]].set(largest)


def shard_levels(own_key, extent, split, smallest, top_value):
    gain = 1.0
    for dim, parts in split:
        heights = jax.random.uniform(jax.random.fold_in(jax.random.fold_in(own_key, 6), dim), (parts,), jnp.float32, smallest / len(split), top_value / len(split))
        gain = gain * jnp.repeat(jnp.exp(heights), extent[dim] // parts).reshape((-1,) + (1,) * (len(extent) - 1 - dim))
    return gain


def centred(key, dims, scale, most, cuts=(), held_as=jnp.bfloat16):
    values = scale * jax.random.normal(key, dims, jnp.float32)
    if cuts:
        values = values * shard_levels(key, dims, cuts, -0.22, 0.18)
    return jnp.clip(values, -most, most).astype(held_as)


def setup_inputs(seed: int = 0) -> dict:
    key_of = jax.random.split(jax.random.key(seed), 7)
    queries = centred(key_of[0], (SEQS, SEQLEN, HEADS * HEAD_DIM), 1.0, 6.0, ((0, 8), (1, 64)))
    keys = centred(key_of[1], (SEQS, SEQLEN, HEADS * HEAD_DIM), 1.0, 6.0, ((0, 8), (1, 64)))
    values = centred(key_of[2], (SEQS, SEQLEN, HEADS * HEAD_DIM), 1.0, 6.0, ((0, 8), (1, 64)))
    out_grad = centred(key_of[3], (SEQS, SEQLEN, HEADS * HEAD_DIM), 1.0, 6.0, ((0, 8), (1, 64)))
    q_gain = jnp.clip(1.0 + 0.15 * jax.random.normal(key_of[4], (HEADS * HEAD_DIM,), jnp.float32), 0.25, 1.75)
    offsets = touch_ends(jax.random.randint(key_of[5], (SEQS, N_CTX), 0, 131072), jax.random.fold_in(key_of[5], 1), 0, 131071).astype(jnp.int32)
    return dict(queries=queries, keys=keys, values=values, out_grad=out_grad, q_gain=q_gain, offsets=offsets)


def rotate(field, position, sign):
    half = field.shape[-1] // 2
    freqs = jnp.power(jnp.float32(500000.0), -(2.0 * jnp.arange(half, dtype=jnp.float32)) / field.shape[-1])
    angle = position.astype(jnp.float32)[:, None] * freqs[None, :]
    cosine = jnp.cos(angle)[:, None, :]
    sine = sign * jnp.sin(angle)[:, None, :]
    first = field[..., :half]
    second = field[..., half:]
    return jnp.concatenate([first * cosine - second * sine, second * cosine + first * sine], axis=-1)


def block_grads(query_blk, key_blk, value_blk, grad_blk, state_blk, back_blk, scale):
    rows = query_blk.shape[0]
    causal = jnp.arange(rows)[:, None] >= jnp.arange(rows)[None, :]
    qf = query_blk.astype(jnp.float32)
    kf = key_blk.astype(jnp.float32)
    vf = value_blk.astype(jnp.float32)
    of = grad_blk.astype(jnp.float32)
    scores = jnp.einsum('thd,shd->hts', qf, kf)
    attn = jnp.where(causal[None], scale * scores, 0.0).astype(jnp.bfloat16).astype(jnp.float32)
    dscores = jnp.einsum('the,she->hts', of, vf)
    dattn = jnp.where(causal[None], scale * dscores, 0.0).astype(jnp.bfloat16).astype(jnp.float32)
    state_low = state_blk.astype(jnp.bfloat16).astype(jnp.float32)
    back_low = back_blk.astype(jnp.bfloat16).astype(jnp.float32)
    dquery = jnp.einsum('hts,shd->thd', dattn, kf) + scale * jnp.einsum('the,hde->thd', of, state_low)
    dkey = jnp.einsum('hts,thd->shd', dattn, qf) + scale * jnp.einsum('she,hde->shd', vf, back_low)
    dvalue = jnp.einsum('hts,the->she', attn, of) + scale * jnp.einsum('shd,hde->she', kf, back_low)
    return dquery, dkey, dvalue


def shard_grads(query_rot, key_rot, value_rows, grad_rows, state_in, back_in, scale):
    rows = query_rot.shape[0]
    nblocks = rows // BLOCK
    shape = (nblocks, BLOCK, HEADS, HEAD_DIM)
    qb = query_rot.reshape(shape)
    kb = key_rot.reshape(shape)
    vb = value_rows.reshape(shape)
    ob = grad_rows.reshape(shape)
    kvb = jnp.einsum('nthd,nthe->nhde', kb.astype(jnp.float32), vb.astype(jnp.float32))
    qob = jnp.einsum('nthd,nthe->nhde', qb.astype(jnp.float32), ob.astype(jnp.float32))
    empty = jnp.zeros((1, HEADS, HEAD_DIM, HEAD_DIM), jnp.float32)
    forward_sum = jnp.concatenate([empty, jnp.cumsum(kvb, axis=0)[:-1]], axis=0)
    backward_sum = jnp.concatenate([jnp.cumsum(qob[::-1], axis=0)[::-1][1:], empty], axis=0)
    states = state_in[None] + forward_sum
    backs = back_in[None] + backward_sum
    dquery, dkey, dvalue = lax.map(lambda item: block_grads(*item, scale), (qb, kb, vb, ob, states, backs))
    flat = (rows, HEADS, HEAD_DIM)
    return dquery.reshape(flat), dkey.reshape(flat), dvalue.reshape(flat)


def reference(queries, keys, values, out_grad, q_gain, offsets):
    width = HEADS * HEAD_DIM
    scale = (HEAD_DIM * SEQLEN) ** -0.5

    def one_sequence(item):
        query_seq, key_seq, value_seq, grad_seq, offset_seq = item
        position = (offset_seq[:, None] + jnp.arange(TOK_DEV, dtype=jnp.int32)[None, :]).reshape(-1)
        query_float = query_seq.astype(jnp.float32)
        query_rot = rotate((query_float * q_gain).reshape(SEQLEN, HEADS, HEAD_DIM), position, 1.0).astype(jnp.bfloat16)
        key_rot = rotate(key_seq.astype(jnp.float32).reshape(SEQLEN, HEADS, HEAD_DIM), position, 1.0).astype(jnp.bfloat16)
        shape = (N_CTX, TOK_DEV, HEADS, HEAD_DIM)
        qs = query_rot.reshape(shape)
        ks = key_rot.reshape(shape)
        vs = value_seq.reshape(shape)
        gs = grad_seq.reshape(shape)
        kv_shard = jnp.einsum('cthd,cthe->chde', ks.astype(jnp.float32), vs.astype(jnp.float32))
        qo_shard = jnp.einsum('cthd,cthe->chde', qs.astype(jnp.float32), gs.astype(jnp.float32))
        empty = jnp.zeros((1, HEADS, HEAD_DIM, HEAD_DIM), jnp.float32)
        state_in = jnp.concatenate([empty, jnp.cumsum(kv_shard, axis=0)[:-1]], axis=0)
        back_in = jnp.concatenate([jnp.cumsum(qo_shard[::-1], axis=0)[::-1][1:], empty], axis=0)
        dquery, dkey, dvalue = lax.map(lambda part: shard_grads(*part, scale), (qs, ks, vs, gs, state_in, back_in))
        flat = (SEQLEN, HEADS, HEAD_DIM)
        dqs = rotate(dquery.reshape(flat), position, -1.0).reshape(SEQLEN, width)
        dks = rotate(dkey.reshape(flat), position, -1.0).reshape(SEQLEN, width)
        gain_part = jnp.sum(dqs * query_float, axis=0)
        return ((dqs * q_gain).astype(jnp.bfloat16), dks.astype(jnp.bfloat16),
                dvalue.reshape(SEQLEN, width).astype(jnp.bfloat16), gain_part)

    grad_queries, grad_keys, grad_values, gain_parts = lax.map(one_sequence, (queries, keys, values, out_grad, offsets))
    grad_gain = jnp.sum(gain_parts, axis=0) * ((SEQS * SEQLEN) ** -0.5)
    return grad_queries, grad_keys, grad_values, grad_gain
```

```python
import functools

import jax
import jax.numpy as jnp
import numpy as np
from jax import lax
from jax.experimental import pallas as pl
from jax.experimental.pallas import tpu as pltpu
from jax.sharding import PartitionSpec as P

HEADS = 2
DIM = 128
HALF = 64
ROWS = 512
BASE = 500000.0
LOW, MIDDLE, HIGH = 32, 64, 65
TABLE = HIGH + MIDDLE + LOW
TABLE_ROWS = 168
PIECE = 16


def rotary_tables():
    freqs = np.power(BASE, -2.0 * np.arange(HALF) / DIM).astype(np.float32).astype(np.float64)
    steps = np.concatenate([np.arange(HIGH) * 2048, np.arange(MIDDLE) * 32, np.arange(LOW)])
    angle = np.zeros((TABLE_ROWS, HALF))
    angle[:TABLE] = steps[:, None] * freqs[None, :]
    cosine, sine = np.cos(angle), np.sin(angle)
    return (
        np.concatenate([cosine, cosine], axis=1).astype(np.float32),
        np.concatenate([-sine, sine], axis=1).astype(np.float32),
    )


def dot(a, b, ca, cb):
    return lax.dot_general(a, b, (((ca,), (cb,)), ((), ())), preferred_element_type=jnp.float32)


def swap(x):
    return pltpu.roll(x, HALF, 1)


def states_kernel(off_ref, ctab_ref, stab_ref, q_ref, k_ref, v_ref, g_ref, send_ref, krot_ref, cos_ref, sin_ref):
    offset = off_ref[0, 0]
    high, middle, low = offset // 2048, (offset // 32) % 64, offset % 32

    def row(at):
        return ctab_ref[pl.ds(at, 1), :], stab_ref[pl.ds(at, 1), :]

    def add(left, right):
        (ca, sa), (cb, sb) = left, right
        return ca * cb - sa * sb, sa * cb + ca * sb

    start = add(add(row(high), row(HIGH + middle)), row(HIGH + MIDDLE + low))
    lows = (
        ctab_ref[HIGH + MIDDLE : HIGH + MIDDLE + LOW, :],
        stab_ref[HIGH + MIDDLE : HIGH + MIDDLE + LOW, :],
    )
    for block in range(ROWS // LOW):
        here = add(start, row(HIGH + block))
        cosine, sine = add(here, lows)
        cos_ref[block * LOW : (block + 1) * LOW, :] = cosine
        sin_ref[block * LOW : (block + 1) * LOW, :] = sine
    cosine, sine = cos_ref[...], sin_ref[...]
    for head in range(HEADS):
        lanes = slice(head * DIM, (head + 1) * DIM)
        q = q_ref[0, :, lanes].astype(jnp.float32)
        k = k_ref[0, :, lanes].astype(jnp.float32)
        krot = (k * cosine + swap(k) * sine).astype(jnp.bfloat16)
        krot_ref[:, lanes] = krot
        kv = dot(krot, v_ref[0, :, lanes], 0, 0)
        g = g_ref[0, :, lanes]
        qcos = dot((q * cosine).astype(jnp.bfloat16), g, 0, 0)
        qsin = dot((q * -sine).astype(jnp.bfloat16), g, 0, 0)
        for half in range(2):
            at = 2 * head + half
            rows = slice(half * HALF, (half + 1) * HALF)
            other = slice((1 - half) * HALF, (2 - half) * HALF)
            send_ref[:, at, :] = kv[rows]
            send_ref[:, 4 + at, :] = kv[rows]
            send_ref[:, 8 + at, :] = qcos[rows]
            send_ref[:, 12 + at, :] = qsin[other]


def local_kernel(
    scale, gain_ref, cos_ref, sin_ref, q_ref, krot_ref, v_ref, g_ref, dq_ref, dk_ref, dv_ref, part_ref
):
    cosine, sine = cos_ref[...], sin_ref[...]
    causal = lax.broadcasted_iota(jnp.int32, (ROWS, ROWS), 0) >= lax.broadcasted_iota(
        jnp.int32, (ROWS, ROWS), 1
    )
    part_ref[...] = jnp.zeros_like(part_ref)
    for head in range(HEADS):
        lanes = slice(head * DIM, (head + 1) * DIM)
        q = q_ref[0, :, lanes].astype(jnp.float32)
        scaled = q * gain_ref[:, lanes]
        qrot = (scaled * cosine + swap(scaled) * sine).astype(jnp.bfloat16)
        krot = krot_ref[:, lanes]
        v = v_ref[0, :, lanes]
        g = g_ref[0, :, lanes]
        attn = jnp.where(causal, scale * dot(qrot, krot, 1, 1), 0.0).astype(jnp.bfloat16)
        dattn = jnp.where(causal, scale * dot(g, v, 1, 1), 0.0).astype(jnp.bfloat16)
        dv_ref[:, lanes] = dot(attn, g, 0, 0)
        dk = dot(dattn, qrot, 0, 0)
        dk_ref[:, lanes] = dk * cosine - swap(dk) * sine
        dq = dot(dattn, krot, 1, 0)
        dq = dq * cosine - swap(dq) * sine
        dq_ref[:, lanes] = dq
        part_ref[head : head + 1, :] = jnp.sum(dq * q, axis=0, keepdims=True)


def scan_kernel(scale, axis, gain_ref, recv_ref, part_ref, send_ref):
    count = recv_ref.shape[0]
    mine = lax.axis_index(axis)
    rows = lax.broadcasted_iota(jnp.int32, (8, DIM), 0)
    gains = [gain_ref[half * HALF + mine] for half in range(4)]
    weight = jnp.zeros((8, DIM), jnp.float32)
    for at, source in enumerate((0, 1, 2, 3, 1, 0, 3, 2)):
        weight = jnp.where(rows == at, gains[source], weight)

    before = jnp.zeros((8, DIM), jnp.float32)
    products = jnp.zeros((8, DIM), jnp.float32)
    for shard in range(count):
        send_ref[shard, 0:8, :] = before
        products += before * recv_ref[shard, 8:16, :]
        before += recv_ref[shard, 0:8, :]
    after = jnp.zeros((8, DIM), jnp.float32)
    for shard in reversed(range(count)):
        back = after * weight
        back = back + pltpu.roll(back, 4, 0)
        send_ref[shard, 0:8, :] = jnp.where(rows < 4, send_ref[shard, 0:8, :], back)
        after += recv_ref[shard, 8:16, :]

    sums = scale * jnp.sum(products, axis=1, keepdims=True)
    lane = lax.broadcasted_iota(jnp.int32, (8, DIM), 1)
    part = part_ref[...]
    for head in range(HEADS):
        for half in range(2):
            at = 2 * head + half
            other = 4 + 2 * head + 1 - half
            value = sums[at : at + 1] + sums[other : other + 1]
            hit = (rows == head) & (lane == mine + half * HALF)
            part = part + jnp.where(hit, value, 0.0)
    for shard in range(count):
        send_ref[shard, 8:16, :] = part


def gain_kernel(recv_ref, out_ref):
    out_ref[...] = jnp.sum(recv_ref[:, 8:16, :], axis=0)


def final_kernel(
    scale, gain_ref, cos_ref, sin_ref, krot_ref, v_ref, g_ref, dq_ref, dk_ref, dv_ref, recv_ref,
    gq_ref, gk_ref, gv_ref,
):
    cosine, sine = cos_ref[...], sin_ref[...]
    for head in range(HEADS):
        lanes = slice(head * DIM, (head + 1) * DIM)

        def matrix(first):
            return jnp.concatenate(
                [recv_ref[:, first, :], recv_ref[:, first + 1, :]], axis=0
            ).astype(jnp.bfloat16)

        state = matrix(2 * head)
        back = matrix(4 + 2 * head)
        dq = scale * dot(g_ref[0, :, lanes], state, 1, 1)
        dq = dq_ref[:, lanes] + (dq * cosine - swap(dq) * sine)
        gq_ref[0, :, lanes] = (dq * gain_ref[:, lanes]).astype(jnp.bfloat16)
        dk = scale * dot(v_ref[0, :, lanes], back, 1, 1)
        gk_ref[0, :, lanes] = (dk_ref[:, lanes] + (dk * cosine - swap(dk) * sine)).astype(jnp.bfloat16)
        dv = scale * dot(krot_ref[:, lanes], back, 1, 0)
        gv_ref[0, :, lanes] = (dv_ref[:, lanes] + dv).astype(jnp.bfloat16)


def total_kernel(factor, parts_ref, out_ref):
    out_ref[...] = jnp.sum(parts_ref[...], axis=0) * factor


VMEM = pl.BlockSpec(memory_space=pltpu.VMEM)
SMEM = pl.BlockSpec(memory_space=pltpu.SMEM)
PARAMS = pltpu.CompilerParams(vmem_limit_bytes=40 * 1024 * 1024)


def shape(*dims, dtype=jnp.float32):
    return jax.ShapeDtypeStruct(dims, dtype)


def local(queries, keys, values, out_grad, q_gain, offsets):
    rows, width = queries.shape[1], queries.shape[2]
    shards = lax.axis_size("ctx")
    all_tokens = rows * shards * lax.axis_size("dp")
    scale = float((DIM * rows * shards) ** (-0.5))
    cos_table, sin_table = rotary_tables()
    gain_row = q_gain.reshape(1, width)

    sent, krot, cosine, sine = pl.pallas_call(
        states_kernel,
        out_shape=(
            shape(shards, PIECE, DIM),
            shape(rows, width, dtype=jnp.bfloat16),
            shape(rows, DIM),
            shape(rows, DIM),
        ),
        in_specs=[SMEM] + [VMEM] * 6,
        out_specs=(VMEM,) * 4,
        compiler_params=PARAMS,
        name="states",
    )(offsets, jnp.asarray(cos_table), jnp.asarray(sin_table), queries, keys, values, out_grad)

    received = lax.all_to_all(sent, "ctx", 0, 0, tiled=True)

    dq, dk, dv, part = pl.pallas_call(
        functools.partial(local_kernel, scale),
        out_shape=(shape(rows, width), shape(rows, width), shape(rows, width), shape(8, DIM)),
        in_specs=[VMEM] * 7,
        out_specs=(VMEM,) * 4,
        compiler_params=PARAMS,
        name="local_grads",
    )(gain_row, cosine, sine, queries, krot, values, out_grad)

    scanned = pl.pallas_call(
        functools.partial(scan_kernel, scale, "ctx"),
        out_shape=shape(shards, PIECE, DIM),
        in_specs=[SMEM, VMEM, VMEM],
        out_specs=VMEM,
        compiler_params=PARAMS,
        name="scan",
    )(q_gain, received, part)

    states = lax.all_to_all(scanned, "ctx", 0, 0, tiled=True)

    gain_part = pl.pallas_call(
        gain_kernel,
        out_shape=shape(8, DIM),
        in_specs=[VMEM],
        out_specs=VMEM,
        compiler_params=PARAMS,
        name="gain_part",
    )(states)
    gathered = lax.all_gather(gain_part, "dp")

    grad_queries, grad_keys, grad_values = pl.pallas_call(
        functools.partial(final_kernel, scale),
        out_shape=(shape(1, rows, width, dtype=jnp.bfloat16),) * 3,
        in_specs=[VMEM] * 10,
        out_specs=(VMEM,) * 3,
        compiler_params=PARAMS,
        name="final",
    )(gain_row, cosine, sine, krot, values, out_grad, dq, dk, dv, states)

    total = pl.pallas_call(
        functools.partial(total_kernel, float(all_tokens ** (-0.5))),
        out_shape=shape(8, DIM),
        in_specs=[VMEM],
        out_specs=VMEM,
        name="gain_total",
    )(gathered)
    grad_gain = total[:HEADS].reshape(width)
    return grad_queries, grad_keys, grad_values, grad_gain


def solution(mesh):
    rows = P("dp", "ctx", None)
    return jax.shard_map(
        local,
        mesh=mesh,
        in_specs=(rows, rows, rows, rows, P(), P("dp", "ctx")),
        out_specs=(rows, rows, rows, P()),
        check_vma=False,
    )
```

```python
import functools

import jax
import jax.numpy as jnp
import numpy as np
from jax import lax
from jax.experimental import pallas as pl
from jax.experimental.pallas import tpu as pltpu
from jax.sharding import PartitionSpec as P

HEADS = 2
DIM = 128
HALF = 64
ROWS = 512
BASE = 500000.0
LOW, MIDDLE, HIGH = 32, 64, 65
TABLE = HIGH + MIDDLE + LOW
TABLE_ROWS = 168
SEND = 12
BACK = 10


def rotary_tables():
    freqs = np.power(BASE, -2.0 * np.arange(HALF) / DIM).astype(np.float32).astype(np.float64)
    steps = np.concatenate([np.arange(HIGH) * 2048, np.arange(MIDDLE) * 32, np.arange(LOW)])
    angle = np.zeros((TABLE_ROWS, HALF))
    angle[:TABLE] = steps[:, None] * freqs[None, :]
    cosine, sine = np.cos(angle), np.sin(angle)
    return (
        np.concatenate([cosine, cosine], axis=1).astype(np.float32),
        np.concatenate([-sine, sine], axis=1).astype(np.float32),
    )


def dot(a, b, ca, cb):
    return lax.dot_general(a, b, (((ca,), (cb,)), ((), ())), preferred_element_type=jnp.float32)


def swap(x):
    return pltpu.roll(x, HALF, 1)


def states_kernel(
    off_ref, ctab_hbm, stab_hbm, q_hbm, k_hbm, v_hbm, g_hbm, send_ref, krot_ref, cos_ref, sin_ref,
    ctab_ref, stab_ref, q_ref, k_ref, v_ref, g_ref, sems,
):
    pairs = (
        (ctab_hbm, ctab_ref),
        (stab_hbm, stab_ref),
        (k_hbm, k_ref),
        (v_hbm, v_ref),
        (q_hbm, q_ref),
        (g_hbm, g_ref),
    )
    copies = [pltpu.make_async_copy(src, dst, sems.at[i]) for i, (src, dst) in enumerate(pairs)]
    for copy in copies:
        copy.start()
    for copy in copies[:2]:
        copy.wait()
    offset = off_ref[0, 0]
    high, middle, low = offset // 2048, (offset // 32) % 64, offset % 32

    def row(at):
        return ctab_ref[pl.ds(at, 1), :], stab_ref[pl.ds(at, 1), :]

    def add(left, right):
        (ca, sa), (cb, sb) = left, right
        return ca * cb - sa * sb, sa * cb + ca * sb

    start = add(add(row(high), row(HIGH + middle)), row(HIGH + MIDDLE + low))
    lows = (
        ctab_ref[HIGH + MIDDLE : HIGH + MIDDLE + LOW, :],
        stab_ref[HIGH + MIDDLE : HIGH + MIDDLE + LOW, :],
    )
    for block in range(ROWS // LOW):
        here = add(start, row(HIGH + block))
        cosine, sine = add(here, lows)
        cos_ref[block * LOW : (block + 1) * LOW, :] = cosine
        sin_ref[block * LOW : (block + 1) * LOW, :] = sine
    cosine, sine = cos_ref[...], sin_ref[...]
    for copy in copies[2:]:
        copy.wait()
    for head in range(HEADS):
        lanes = slice(head * DIM, (head + 1) * DIM)
        k = k_ref[0, :, lanes].astype(jnp.float32)
        krot = (k * cosine + swap(k) * sine).astype(jnp.bfloat16)
        krot_ref[:, lanes] = krot
        kv = dot(krot, v_ref[0, :, lanes], 0, 0)
        q = q_ref[0, :, lanes].astype(jnp.float32)
        g = g_ref[0, :, lanes]
        qcos = dot((q * cosine).astype(jnp.bfloat16), g, 0, 0)
        qsin = dot((q * -sine).astype(jnp.bfloat16), g, 0, 0)
        for half in range(2):
            at = 2 * head + half
            rows = slice(half * HALF, (half + 1) * HALF)
            other = slice((1 - half) * HALF, (2 - half) * HALF)
            send_ref[pl.ds(at, HALF, stride=SEND), :] = kv[rows]
            send_ref[pl.ds(4 + at, HALF, stride=SEND), :] = qcos[rows]
            send_ref[pl.ds(8 + at, HALF, stride=SEND), :] = qsin[other]


def local_kernel(
    scale, gain_ref, cos_ref, sin_ref, q_ref, krot_ref, v_ref, g_ref, dq_ref, dk_ref, dv_ref, part_ref
):
    cosine, sine = cos_ref[...], sin_ref[...]
    causal = lax.broadcasted_iota(jnp.int32, (ROWS, ROWS), 0) >= lax.broadcasted_iota(
        jnp.int32, (ROWS, ROWS), 1
    )
    part_ref[...] = jnp.zeros_like(part_ref)
    for head in range(HEADS):
        lanes = slice(head * DIM, (head + 1) * DIM)
        q = q_ref[0, :, lanes].astype(jnp.float32)
        scaled = q * gain_ref[:, lanes]
        qrot = (scaled * cosine + swap(scaled) * sine).astype(jnp.bfloat16)
        krot = krot_ref[:, lanes]
        v = v_ref[0, :, lanes]
        g = g_ref[0, :, lanes]
        attn = jnp.where(causal, scale * dot(qrot, krot, 1, 1), 0.0).astype(jnp.bfloat16)
        dattn = jnp.where(causal, scale * dot(g, v, 1, 1), 0.0).astype(jnp.bfloat16)
        dv_ref[:, lanes] = dot(attn, g, 0, 0)
        dk = dot(dattn, qrot, 0, 0)
        dk_ref[:, lanes] = dk * cosine - swap(dk) * sine
        dq = dot(dattn, krot, 1, 0)
        dq = dq * cosine - swap(dq) * sine
        dq_ref[:, lanes] = dq
        part_ref[head : head + 1, :] = jnp.sum(dq * q, axis=0, keepdims=True)


def scan_kernel(scale, axis, count, gain_ref, recv_ref, part_ref, send_ref):
    mine = lax.axis_index(axis)
    rows = lax.broadcasted_iota(jnp.int32, (8, DIM), 0)
    gains = [gain_ref[half * HALF + mine] for half in range(4)]
    weight = jnp.zeros((8, DIM), jnp.float32)
    for at, source in enumerate((0, 1, 2, 3, 1, 0, 3, 2)):
        weight = jnp.where(rows == at, gains[source], weight)

    before = jnp.zeros((8, DIM), jnp.float32)
    products = jnp.zeros((8, DIM), jnp.float32)
    for shard in range(count):
        twice = jnp.where(rows < 4, before, pltpu.roll(before, 4, 0))
        send_ref[BACK * shard : BACK * shard + 8, :] = twice
        products += twice * recv_ref[SEND * shard + 4 : SEND * shard + 12, :]
        before += recv_ref[SEND * shard : SEND * shard + 8, :]
    after = jnp.zeros((8, DIM), jnp.float32)
    for shard in reversed(range(count)):
        back = after * weight
        back = back + pltpu.roll(back, 4, 0)
        send_ref[BACK * shard + 4 : BACK * shard + 8, :] = back[:4]
        after += recv_ref[SEND * shard + 4 : SEND * shard + 12, :]

    sums = scale * jnp.sum(products, axis=1, keepdims=True)
    lane = lax.broadcasted_iota(jnp.int32, (8, DIM), 1)
    part = part_ref[...]
    for head in range(HEADS):
        for half in range(2):
            at = 2 * head + half
            other = 4 + 2 * head + 1 - half
            value = sums[at : at + 1] + sums[other : other + 1]
            hit = (rows == head) & (lane == mine + half * HALF)
            part = part + jnp.where(hit, value, 0.0)
    for shard in range(count):
        send_ref[BACK * shard + 8 : BACK * shard + 10, :] = part[:HEADS]


def gain_kernel(count, recv_ref, out_ref):
    copies = out_ref.shape[0] // HEADS
    for head in range(HEADS):
        part = jnp.sum(recv_ref[pl.ds(8 + head, count, stride=BACK), :], axis=0, keepdims=True)
        for copy in range(copies):
            out_ref[HEADS * copy + head : HEADS * copy + head + 1, :] = part


def final_kernel(
    scale, factor, gain_ref, cos_ref, sin_ref, krot_ref, v_ref, g_ref, dq_ref, dk_ref, dv_ref, recv_ref, parts_ref,
    gq_ref, gk_ref, gv_ref, total_ref,
):
    cosine, sine = cos_ref[...], sin_ref[...]
    for head in range(HEADS):
        lanes = slice(head * DIM, (head + 1) * DIM)
        parts = parts_ref[pl.ds(head, parts_ref.shape[0] // HEADS, stride=HEADS), :]
        total_ref[:, lanes] = jnp.sum(parts, axis=0, keepdims=True) * factor

        def matrix(first):
            halves = [recv_ref[pl.ds(first + half, HALF, stride=BACK), :] for half in range(2)]
            return jnp.concatenate(halves, axis=0).astype(jnp.bfloat16)

        state = matrix(2 * head)
        back = matrix(4 + 2 * head)
        dq = scale * dot(g_ref[0, :, lanes], state, 1, 1)
        dq = dq_ref[:, lanes] + (dq * cosine - swap(dq) * sine)
        gq_ref[0, :, lanes] = (dq * gain_ref[:, lanes]).astype(jnp.bfloat16)
        dk = scale * dot(v_ref[0, :, lanes], back, 1, 1)
        gk_ref[0, :, lanes] = (dk_ref[:, lanes] + (dk * cosine - swap(dk) * sine)).astype(jnp.bfloat16)
        dv = scale * dot(krot_ref[:, lanes], back, 1, 0)
        gv_ref[0, :, lanes] = (dv_ref[:, lanes] + dv).astype(jnp.bfloat16)


VMEM = pl.BlockSpec(memory_space=pltpu.VMEM)
SMEM = pl.BlockSpec(memory_space=pltpu.SMEM)
HBM = pl.BlockSpec(memory_space=pltpu.HBM)
PARAMS = pltpu.CompilerParams(vmem_limit_bytes=24 * 1024 * 1024)


def shape(*dims, dtype=jnp.float32):
    return jax.ShapeDtypeStruct(dims, dtype)


def exchange(rows, axis):
    count = lax.axis_size(axis)
    pieces = rows.reshape(count, 1, rows.size // count)
    return lax.all_to_all(pieces, axis, 0, 0, tiled=True).reshape(rows.shape)


def local(queries, keys, values, out_grad, q_gain, offsets):
    rows, width = queries.shape[1], queries.shape[2]
    shards, groups = lax.axis_size("ctx"), lax.axis_size("dp")
    scale = float((DIM * rows * shards) ** (-0.5))
    factor = float((rows * shards * groups) ** (-0.5))
    cos_table, sin_table = rotary_tables()
    gain_row = q_gain.reshape(1, width)
    tokens = queries.shape

    sent, krot, cosine, sine = pl.pallas_call(
        states_kernel,
        out_shape=(
            shape(shards * SEND, DIM),
            shape(rows, width, dtype=jnp.bfloat16),
            shape(rows, DIM),
            shape(rows, DIM),
        ),
        in_specs=[SMEM] + [HBM] * 6,
        out_specs=(VMEM,) * 4,
        scratch_shapes=[
            pltpu.VMEM(cos_table.shape, jnp.float32),
            pltpu.VMEM(cos_table.shape, jnp.float32),
            pltpu.VMEM(tokens, jnp.bfloat16),
            pltpu.VMEM(tokens, jnp.bfloat16),
            pltpu.VMEM(tokens, jnp.bfloat16),
            pltpu.VMEM(tokens, jnp.bfloat16),
            pltpu.SemaphoreType.DMA((6,)),
        ],
        compiler_params=PARAMS,
        name="states",
    )(
        offsets,
        *(
            pltpu.with_memory_space_constraint(x, pltpu.HBM)
            for x in (jnp.asarray(cos_table), jnp.asarray(sin_table), queries, keys, values, out_grad)
        )
    )

    received = exchange(sent, "ctx")

    dq, dk, dv, part = pl.pallas_call(
        functools.partial(local_kernel, scale),
        out_shape=(shape(rows, width), shape(rows, width), shape(rows, width), shape(8, DIM)),
        in_specs=[VMEM] * 7,
        out_specs=(VMEM,) * 4,
        compiler_params=PARAMS,
        name="local_grads",
    )(gain_row, cosine, sine, queries, krot, values, out_grad)

    scanned = pl.pallas_call(
        functools.partial(scan_kernel, scale, "ctx", shards),
        out_shape=shape(shards * BACK, DIM),
        in_specs=[SMEM, VMEM, VMEM],
        out_specs=VMEM,
        compiler_params=PARAMS,
        name="scan",
    )(q_gain, received, part)

    states = exchange(scanned, "ctx")

    gain_part = pl.pallas_call(
        functools.partial(gain_kernel, shards),
        out_shape=shape(groups * HEADS, DIM),
        in_specs=[VMEM],
        out_specs=VMEM,
        compiler_params=PARAMS,
        name="gain_part",
    )(states)
    gain_parts = exchange(gain_part, "dp")

    grad_queries, grad_keys, grad_values, grad_gain = pl.pallas_call(
        functools.partial(final_kernel, scale, factor),
        out_shape=(shape(*tokens, dtype=jnp.bfloat16),) * 3 + (shape(1, width),),
        in_specs=[VMEM] * 11,
        out_specs=(VMEM,) * 4,
        compiler_params=PARAMS,
        name="final",
    )(gain_row, cosine, sine, krot, values, out_grad, dq, dk, dv, states, gain_parts)
    return grad_queries, grad_keys, grad_values, grad_gain.reshape(width)


def solution(mesh):
    rows = P("dp", "ctx", None)
    return jax.shard_map(
        local,
        mesh=mesh,
        in_specs=(rows, rows, rows, rows, P(), P("dp", "ctx")),
        out_specs=(rows, rows, rows, P()),
        check_vma=False,
    )
```

```python
import functools

import jax
import jax.numpy as jnp
import numpy as np
from jax import lax
from jax.experimental import pallas as pl
from jax.experimental.pallas import tpu as pltpu
from jax.sharding import PartitionSpec as P

HEADS = 2
DIM = 128
HALF = 64
ROWS = 512
BASE = 500000.0
LOW, MIDDLE, HIGH = 32, 64, 65
TABLE = HIGH + MIDDLE + LOW
TABLE_ROWS = 168
SEND = 12
BACK = 10
SIDE = 8
FIRST = (5, 4)


def rotary_tables():
    freqs = np.power(BASE, -2.0 * np.arange(HALF) / DIM).astype(np.float32).astype(np.float64)
    steps = np.concatenate([np.arange(HIGH) * 2048, np.arange(MIDDLE) * 32, np.arange(LOW)])
    angle = np.zeros((TABLE_ROWS, HALF))
    angle[:TABLE] = steps[:, None] * freqs[None, :]
    cosine, sine = np.cos(angle), np.sin(angle)
    return (
        np.concatenate([cosine, cosine], axis=1).astype(np.float32),
        np.concatenate([-sine, sine], axis=1).astype(np.float32),
    )


def dot(a, b, ca, cb):
    return lax.dot_general(a, b, (((ca,), (cb,)), ((), ())), preferred_element_type=jnp.float32)


def swap(x):
    return pltpu.roll(x, HALF, 1)


def states_kernel(
    off_ref, ctab_hbm, stab_hbm, q_hbm, k_hbm, v_hbm, g_hbm, send_ref, krot_ref, cos_ref, sin_ref,
    ctab_ref, stab_ref, q_ref, k_ref, v_ref, g_ref, sems,
):
    pairs = (
        (ctab_hbm, ctab_ref),
        (stab_hbm, stab_ref),
        (k_hbm, k_ref),
        (v_hbm, v_ref),
        (q_hbm, q_ref),
        (g_hbm, g_ref),
    )
    copies = [pltpu.make_async_copy(src, dst, sems.at[i]) for i, (src, dst) in enumerate(pairs)]
    for copy in copies:
        copy.start()
    for copy in copies[:2]:
        copy.wait()
    offset = off_ref[0, 0]
    high, middle, low = offset // 2048, (offset // 32) % 64, offset % 32

    def row(at):
        return ctab_ref[pl.ds(at, 1), :], stab_ref[pl.ds(at, 1), :]

    def add(left, right):
        (ca, sa), (cb, sb) = left, right
        return ca * cb - sa * sb, sa * cb + ca * sb

    start = add(add(row(high), row(HIGH + middle)), row(HIGH + MIDDLE + low))
    lows = (
        ctab_ref[HIGH + MIDDLE : HIGH + MIDDLE + LOW, :],
        stab_ref[HIGH + MIDDLE : HIGH + MIDDLE + LOW, :],
    )
    for block in range(ROWS // LOW):
        here = add(start, row(HIGH + block))
        cosine, sine = add(here, lows)
        cos_ref[block * LOW : (block + 1) * LOW, :] = cosine
        sin_ref[block * LOW : (block + 1) * LOW, :] = sine
    cosine, sine = cos_ref[...], sin_ref[...]
    for copy in copies[2:]:
        copy.wait()
    for head in range(HEADS):
        lanes = slice(head * DIM, (head + 1) * DIM)
        k = k_ref[0, :, lanes].astype(jnp.float32)
        krot = (k * cosine + swap(k) * sine).astype(jnp.bfloat16)
        krot_ref[:, lanes] = krot
        kv = dot(krot, v_ref[0, :, lanes], 0, 0)
        q = q_ref[0, :, lanes].astype(jnp.float32)
        g = g_ref[0, :, lanes]
        qcos = dot((q * cosine).astype(jnp.bfloat16), g, 0, 0)
        qsin = dot((q * -sine).astype(jnp.bfloat16), g, 0, 0)
        for half in range(2):
            at = 2 * head + half
            rows = slice(half * HALF, (half + 1) * HALF)
            other = slice((1 - half) * HALF, (2 - half) * HALF)
            send_ref[pl.ds(at, HALF, stride=SEND), :] = kv[rows]
            send_ref[pl.ds(4 + at, HALF, stride=SEND), :] = qcos[rows]
            send_ref[pl.ds(8 + at, HALF, stride=SEND), :] = qsin[other]


def local_kernel(
    scale, gain_ref, cos_ref, sin_ref, q_ref, krot_ref, v_ref, g_ref, dq_ref, dk_ref, dv_ref, part_ref
):
    cosine, sine = cos_ref[...], sin_ref[...]
    causal = lax.broadcasted_iota(jnp.int32, (ROWS, ROWS), 0) >= lax.broadcasted_iota(
        jnp.int32, (ROWS, ROWS), 1
    )
    part_ref[...] = jnp.zeros_like(part_ref)
    for head in range(HEADS):
        lanes = slice(head * DIM, (head + 1) * DIM)
        q = q_ref[0, :, lanes].astype(jnp.float32)
        scaled = q * gain_ref[:, lanes]
        qrot = (scaled * cosine + swap(scaled) * sine).astype(jnp.bfloat16)
        krot = krot_ref[:, lanes]
        v = v_ref[0, :, lanes]
        g = g_ref[0, :, lanes]
        attn = jnp.where(causal, scale * dot(qrot, krot, 1, 1), 0.0).astype(jnp.bfloat16)
        dattn = jnp.where(causal, scale * dot(g, v, 1, 1), 0.0).astype(jnp.bfloat16)
        dv_ref[:, lanes] = dot(attn, g, 0, 0)
        dk = dot(dattn, qrot, 0, 0)
        dk_ref[:, lanes] = dk * cosine - swap(dk) * sine
        dq = dot(dattn, krot, 1, 0)
        dq = dq * cosine - swap(dq) * sine
        dq_ref[:, lanes] = dq
        part_ref[head : head + 1, :] = jnp.sum(dq * q, axis=0, keepdims=True)


def rank(shard):
    return (shard // SIDE - FIRST[0]) % SIDE * SIDE + (shard % SIDE - FIRST[1]) % SIDE


def scan_kernel(scale, axis, count, gain_ref, recv_ref, part_ref, send_ref):
    index = lax.axis_index(axis)
    mine = lax.rem(lax.div(index, SIDE) + SIDE - FIRST[0], SIDE) * SIDE + lax.rem(
        lax.rem(index, SIDE) + SIDE - FIRST[1], SIDE
    )
    rows = lax.broadcasted_iota(jnp.int32, (8, DIM), 0)
    gains = [gain_ref[half * HALF + mine] for half in range(4)]
    weight = jnp.zeros((8, DIM), jnp.float32)
    for at, source in enumerate((0, 1, 2, 3, 1, 0, 3, 2)):
        weight = jnp.where(rows == at, gains[source], weight)

    before = jnp.zeros((8, DIM), jnp.float32)
    products = jnp.zeros((8, DIM), jnp.float32)
    for shard in range(count):
        source, target = SEND * rank(shard), BACK * rank(shard)
        twice = jnp.where(rows < 4, before, pltpu.roll(before, 4, 0))
        send_ref[target : target + 8, :] = twice
        products += twice * recv_ref[source + 4 : source + 12, :]
        before += recv_ref[source : source + 8, :]
    after = jnp.zeros((8, DIM), jnp.float32)
    for shard in reversed(range(count)):
        source, target = SEND * rank(shard), BACK * rank(shard)
        back = after * weight
        back = back + pltpu.roll(back, 4, 0)
        send_ref[target + 4 : target + 8, :] = back[:4]
        after += recv_ref[source + 4 : source + 12, :]

    sums = scale * jnp.sum(products, axis=1, keepdims=True)
    lane = lax.broadcasted_iota(jnp.int32, (8, DIM), 1)
    part = part_ref[...]
    for head in range(HEADS):
        for half in range(2):
            at = 2 * head + half
            other = 4 + 2 * head + 1 - half
            value = sums[at : at + 1] + sums[other : other + 1]
            hit = (rows == head) & (lane == mine + half * HALF)
            part = part + jnp.where(hit, value, 0.0)
    for shard in range(count):
        send_ref[BACK * shard + 8 : BACK * shard + 10, :] = part[:HEADS]


def gain_kernel(count, recv_ref, out_ref):
    copies = out_ref.shape[0] // HEADS
    for head in range(HEADS):
        part = jnp.sum(recv_ref[pl.ds(8 + head, count, stride=BACK), :], axis=0, keepdims=True)
        for copy in range(copies):
            out_ref[HEADS * copy + head : HEADS * copy + head + 1, :] = part


def final_kernel(
    scale, factor, gain_ref, cos_ref, sin_ref, krot_ref, v_ref, g_ref, dq_ref, dk_ref, dv_ref, recv_ref, parts_ref,
    gq_ref, gk_ref, gv_ref, total_ref,
):
    cosine, sine = cos_ref[...], sin_ref[...]
    for head in range(HEADS):
        lanes = slice(head * DIM, (head + 1) * DIM)
        parts = parts_ref[pl.ds(head, parts_ref.shape[0] // HEADS, stride=HEADS), :]
        total_ref[:, lanes] = jnp.sum(parts, axis=0, keepdims=True) * factor

        def matrix(first):
            halves = [recv_ref[pl.ds(first + half, HALF, stride=BACK), :] for half in range(2)]
            return jnp.concatenate(halves, axis=0).astype(jnp.bfloat16)

        state = matrix(2 * head)
        back = matrix(4 + 2 * head)
        dq = scale * dot(g_ref[0, :, lanes], state, 1, 1)
        dq = dq_ref[:, lanes] + (dq * cosine - swap(dq) * sine)
        gq_ref[0, :, lanes] = (dq * gain_ref[:, lanes]).astype(jnp.bfloat16)
        dk = scale * dot(v_ref[0, :, lanes], back, 1, 1)
        gk_ref[0, :, lanes] = (dk_ref[:, lanes] + (dk * cosine - swap(dk) * sine)).astype(jnp.bfloat16)
        dv = scale * dot(krot_ref[:, lanes], back, 1, 0)
        gv_ref[0, :, lanes] = (dv_ref[:, lanes] + dv).astype(jnp.bfloat16)


VMEM = pl.BlockSpec(memory_space=pltpu.VMEM)
SMEM = pl.BlockSpec(memory_space=pltpu.SMEM)
HBM = pl.BlockSpec(memory_space=pltpu.HBM)
PARAMS = pltpu.CompilerParams(vmem_limit_bytes=24 * 1024 * 1024)


def shape(*dims, dtype=jnp.float32):
    return jax.ShapeDtypeStruct(dims, dtype)


def exchange(rows, axis, order=None):
    count = lax.axis_size(axis)
    pieces = rows.reshape(count, 1, rows.size // count)
    groups = None if order is None else [order]
    return lax.all_to_all(pieces, axis, 0, 0, axis_index_groups=groups, tiled=True).reshape(rows.shape)


def local(queries, keys, values, out_grad, q_gain, offsets):
    rows, width = queries.shape[1], queries.shape[2]
    shards, groups = lax.axis_size("ctx"), lax.axis_size("dp")
    scale = float((DIM * rows * shards) ** (-0.5))
    factor = float((rows * shards * groups) ** (-0.5))
    cos_table, sin_table = rotary_tables()
    gain_row = q_gain.reshape(1, width)
    order = sorted(range(shards), key=rank)
    tokens = queries.shape

    sent, krot, cosine, sine = pl.pallas_call(
        states_kernel,
        out_shape=(
            shape(shards * SEND, DIM),
            shape(rows, width, dtype=jnp.bfloat16),
            shape(rows, DIM),
            shape(rows, DIM),
        ),
        in_specs=[SMEM] + [HBM] * 6,
        out_specs=(VMEM,) * 4,
        scratch_shapes=[
            pltpu.VMEM(cos_table.shape, jnp.float32),
            pltpu.VMEM(cos_table.shape, jnp.float32),
            pltpu.VMEM(tokens, jnp.bfloat16),
            pltpu.VMEM(tokens, jnp.bfloat16),
            pltpu.VMEM(tokens, jnp.bfloat16),
            pltpu.VMEM(tokens, jnp.bfloat16),
            pltpu.SemaphoreType.DMA((6,)),
        ],
        compiler_params=PARAMS,
        name="states",
    )(
        offsets,
        *(
            pltpu.with_memory_space_constraint(x, pltpu.HBM)
            for x in (jnp.asarray(cos_table), jnp.asarray(sin_table), queries, keys, values, out_grad)
        )
    )

    received = exchange(sent, "ctx", order)

    dq, dk, dv, part = pl.pallas_call(
        functools.partial(local_kernel, scale),
        out_shape=(shape(rows, width), shape(rows, width), shape(rows, width), shape(8, DIM)),
        in_specs=[VMEM] * 7,
        out_specs=(VMEM,) * 4,
        compiler_params=PARAMS,
        name="local_grads",
    )(gain_row, cosine, sine, queries, krot, values, out_grad)

    scanned = pl.pallas_call(
        functools.partial(scan_kernel, scale, "ctx", shards),
        out_shape=shape(shards * BACK, DIM),
        in_specs=[SMEM, VMEM, VMEM],
        out_specs=VMEM,
        compiler_params=PARAMS,
        name="scan",
    )(q_gain, received, part)

    states = exchange(scanned, "ctx", order)

    gain_part = pl.pallas_call(
        functools.partial(gain_kernel, shards),
        out_shape=shape(groups * HEADS, DIM),
        in_specs=[VMEM],
        out_specs=VMEM,
        compiler_params=PARAMS,
        name="gain_part",
    )(states)
    gain_parts = exchange(gain_part, "dp")

    grad_queries, grad_keys, grad_values, grad_gain = pl.pallas_call(
        functools.partial(final_kernel, scale, factor),
        out_shape=(shape(*tokens, dtype=jnp.bfloat16),) * 3 + (shape(1, width),),
        in_specs=[VMEM] * 11,
        out_specs=(VMEM,) * 4,
        compiler_params=PARAMS,
        name="final",
    )(gain_row, cosine, sine, krot, values, out_grad, dq, dk, dv, states, gain_parts)
    return grad_queries, grad_keys, grad_values, grad_gain.reshape(width)


def solution(mesh):
    rows = P("dp", "ctx", None)
    return jax.shard_map(
        local,
        mesh=mesh,
        in_specs=(rows, rows, rows, rows, P(), P("dp", "ctx")),
        out_specs=(rows, rows, rows, P()),
        check_vma=False,
    )
```

```python
import functools

import jax
import jax.numpy as jnp
import numpy as np
from jax import lax
from jax.experimental import pallas as pl
from jax.experimental.pallas import tpu as pltpu
from jax.sharding import PartitionSpec as P

HEADS = 2
DIM = 128
HALF = 64
ROWS = 512
BASE = 500000.0
LOW, MIDDLE, HIGH = 32, 64, 65
TABLE = HIGH + MIDDLE + LOW
TABLE_ROWS = 168
SEND = 12
BACK = 10
SIDE = 8
FIRST = (4, 4)
FIRST_DP = 4


def rotary_tables():
    freqs = np.power(BASE, -2.0 * np.arange(HALF) / DIM).astype(np.float32).astype(np.float64)
    steps = np.concatenate([np.arange(HIGH) * 2048, np.arange(MIDDLE) * 32, np.arange(LOW)])
    angle = np.zeros((TABLE_ROWS, HALF))
    angle[:TABLE] = steps[:, None] * freqs[None, :]
    cosine, sine = np.cos(angle), np.sin(angle)
    return (
        np.concatenate([cosine, cosine], axis=1).astype(np.float32),
        np.concatenate([-sine, sine], axis=1).astype(np.float32),
    )


def dot(a, b, ca, cb):
    return lax.dot_general(a, b, (((ca,), (cb,)), ((), ())), preferred_element_type=jnp.float32)


def swap(x):
    return pltpu.roll(x, HALF, 1)


def states_kernel(
    off_ref, ctab_hbm, stab_hbm, q_hbm, k_hbm, v_hbm, g_hbm, send_ref, krot_ref, cos_ref, sin_ref,
    ctab_ref, stab_ref, q_ref, k_ref, v_ref, g_ref, sems,
):
    pairs = (
        (ctab_hbm, ctab_ref),
        (stab_hbm, stab_ref),
        (k_hbm, k_ref),
        (v_hbm, v_ref),
        (q_hbm, q_ref),
        (g_hbm, g_ref),
    )
    copies = [pltpu.make_async_copy(src, dst, sems.at[i]) for i, (src, dst) in enumerate(pairs)]
    for copy in copies:
        copy.start()
    for copy in copies[:2]:
        copy.wait()
    offset = off_ref[0, 0]
    high, middle, low = offset // 2048, (offset // 32) % 64, offset % 32

    def row(at):
        return ctab_ref[pl.ds(at, 1), :], stab_ref[pl.ds(at, 1), :]

    def add(left, right):
        (ca, sa), (cb, sb) = left, right
        return ca * cb - sa * sb, sa * cb + ca * sb

    start = add(add(row(high), row(HIGH + middle)), row(HIGH + MIDDLE + low))
    lows = (
        ctab_ref[HIGH + MIDDLE : HIGH + MIDDLE + LOW, :],
        stab_ref[HIGH + MIDDLE : HIGH + MIDDLE + LOW, :],
    )
    for block in range(ROWS // LOW):
        here = add(start, row(HIGH + block))
        cosine, sine = add(here, lows)
        cos_ref[block * LOW : (block + 1) * LOW, :] = cosine
        sin_ref[block * LOW : (block + 1) * LOW, :] = sine
    cosine, sine = cos_ref[...], sin_ref[...]
    for copy in copies[2:]:
        copy.wait()
    for head in range(HEADS):
        lanes = slice(head * DIM, (head + 1) * DIM)
        k = k_ref[0, :, lanes].astype(jnp.float32)
        krot = (k * cosine + swap(k) * sine).astype(jnp.bfloat16)
        krot_ref[:, lanes] = krot
        kv = dot(v_ref[0, :, lanes], krot, 0, 0)
        q = q_ref[0, :, lanes].astype(jnp.float32)
        pair = jnp.concatenate([q * cosine, q * -sine], axis=1).astype(jnp.bfloat16)
        gq = dot(g_ref[0, :, lanes], pair, 0, 0)
        for half in range(2):
            at = 2 * head + half
            rows = slice(half * HALF, (half + 1) * HALF)
            send_ref[pl.ds(at, HALF, stride=SEND), :] = kv[rows]
            send_ref[pl.ds(4 + at, HALF, stride=SEND), :] = gq[rows, :DIM]
            send_ref[pl.ds(8 + at, HALF, stride=SEND), :] = gq[rows, DIM:]


def local_kernel(
    scale, gain_ref, cos_ref, sin_ref, q_ref, krot_ref, v_ref, g_ref, dq_ref, dk_ref, dv_ref, part_ref
):
    cosine, sine = cos_ref[...], sin_ref[...]
    causal = lax.broadcasted_iota(jnp.int32, (ROWS, ROWS), 0) >= lax.broadcasted_iota(
        jnp.int32, (ROWS, ROWS), 1
    )
    part_ref[...] = jnp.zeros_like(part_ref)
    for head in range(HEADS):
        lanes = slice(head * DIM, (head + 1) * DIM)
        q = q_ref[0, :, lanes].astype(jnp.float32)
        scaled = q * gain_ref[:, lanes]
        qrot = (scaled * cosine + swap(scaled) * sine).astype(jnp.bfloat16)
        krot = krot_ref[:, lanes]
        v = v_ref[0, :, lanes]
        g = g_ref[0, :, lanes]
        attn = jnp.where(causal, scale * dot(qrot, krot, 1, 1), 0.0).astype(jnp.bfloat16)
        dattn = jnp.where(causal, scale * dot(g, v, 1, 1), 0.0).astype(jnp.bfloat16)
        dv_ref[:, lanes] = dot(attn, g, 0, 0)
        dk = dot(dattn, qrot, 0, 0)
        dk_ref[:, lanes] = dk * cosine - swap(dk) * sine
        dq = dot(dattn, krot, 1, 0)
        dq = dq * cosine - swap(dq) * sine
        dq_ref[:, lanes] = dq
        part_ref[head : head + 1, :] = jnp.sum(dq * q, axis=0, keepdims=True)


def rank(shard):
    return (shard // SIDE - FIRST[0]) % SIDE * SIDE + (shard % SIDE - FIRST[1]) % SIDE


def scan_kernel(scale, count, gain_ref, recv_ref, part_ref, send_ref):
    rows = lax.broadcasted_iota(jnp.int32, (8, DIM), 0)
    weight = jnp.where(rows % 4 < 2, gain_ref[:, :DIM], gain_ref[:, DIM:])

    before = jnp.zeros((8, DIM), jnp.float32)
    products = jnp.zeros((8, DIM), jnp.float32)
    for shard in range(count):
        source, target = SEND * rank(shard), BACK * rank(shard)
        twice = jnp.where(rows < 4, before, swap(pltpu.roll(before, 4, 0)))
        send_ref[target : target + 8, :] = twice
        products += twice * recv_ref[source + 4 : source + 12, :]
        before += recv_ref[source : source + 8, :]
    after = jnp.zeros((8, DIM), jnp.float32)
    for shard in reversed(range(count)):
        source, target = SEND * rank(shard), BACK * rank(shard)
        back = after * weight
        back = back + swap(pltpu.roll(back, 4, 0))
        send_ref[target + 4 : target + 8, :] = back[:4]
        after += recv_ref[source + 4 : source + 12, :]

    part = part_ref[...]
    for head in range(HEADS):
        mine = jnp.where(rows % 4 // 2 == head, products, 0.0)
        total = scale * jnp.sum(mine, axis=0, keepdims=True)
        part = part + jnp.where(rows == head, total, 0.0)
    for shard in range(count):
        send_ref[BACK * shard + 8 : BACK * shard + 10, :] = part[:HEADS]


def gain_kernel(count, recv_ref, out_ref):
    copies = out_ref.shape[0] // HEADS
    for head in range(HEADS):
        part = jnp.sum(recv_ref[pl.ds(8 + head, count, stride=BACK), :], axis=0, keepdims=True)
        for copy in range(copies):
            out_ref[HEADS * copy + head : HEADS * copy + head + 1, :] = part


def final_kernel(
    scale, factor, gain_ref, cos_ref, sin_ref, krot_ref, v_ref, g_ref, dq_ref, dk_ref, dv_ref, recv_ref, parts_ref,
    gq_ref, gk_ref, gv_ref, total_ref,
):
    cosine, sine = cos_ref[...], sin_ref[...]
    for head in range(HEADS):
        lanes = slice(head * DIM, (head + 1) * DIM)
        parts = parts_ref[pl.ds(head, parts_ref.shape[0] // HEADS, stride=HEADS), :]
        total_ref[:, lanes] = jnp.sum(parts, axis=0, keepdims=True) * factor

        def matrix(first):
            halves = [recv_ref[pl.ds(first + half, HALF, stride=BACK), :] for half in range(2)]
            return jnp.concatenate(halves, axis=0).astype(jnp.bfloat16)

        state = matrix(2 * head)
        back = matrix(4 + 2 * head)
        dq = scale * dot(g_ref[0, :, lanes], state, 1, 0)
        dq = dq_ref[:, lanes] + (dq * cosine - swap(dq) * sine)
        gq_ref[0, :, lanes] = (dq * gain_ref[:, lanes]).astype(jnp.bfloat16)
        dk = scale * dot(v_ref[0, :, lanes], back, 1, 0)
        gk_ref[0, :, lanes] = (dk_ref[:, lanes] + (dk * cosine - swap(dk) * sine)).astype(jnp.bfloat16)
        dv = scale * dot(krot_ref[:, lanes], back, 1, 1)
        gv_ref[0, :, lanes] = (dv_ref[:, lanes] + dv).astype(jnp.bfloat16)


VMEM = pl.BlockSpec(memory_space=pltpu.VMEM)
SMEM = pl.BlockSpec(memory_space=pltpu.SMEM)
HBM = pl.BlockSpec(memory_space=pltpu.HBM)
PARAMS = pltpu.CompilerParams(vmem_limit_bytes=24 * 1024 * 1024)


def shape(*dims, dtype=jnp.float32):
    return jax.ShapeDtypeStruct(dims, dtype)


def exchange(rows, axis, order=None):
    count = lax.axis_size(axis)
    pieces = rows.reshape(count, 1, rows.size // count)
    groups = None if order is None else [order]
    return lax.all_to_all(pieces, axis, 0, 0, axis_index_groups=groups, tiled=True).reshape(rows.shape)


def local(queries, keys, values, out_grad, q_gain, offsets):
    rows, width = queries.shape[1], queries.shape[2]
    shards, groups = lax.axis_size("ctx"), lax.axis_size("dp")
    scale = float((DIM * rows * shards) ** (-0.5))
    factor = float((rows * shards * groups) ** (-0.5))
    cos_table, sin_table = rotary_tables()
    gain_row = q_gain.reshape(1, width)
    order = sorted(range(shards), key=rank)
    tokens = queries.shape

    sent, krot, cosine, sine = pl.pallas_call(
        states_kernel,
        out_shape=(
            shape(shards * SEND, DIM),
            shape(rows, width, dtype=jnp.bfloat16),
            shape(rows, DIM),
            shape(rows, DIM),
        ),
        in_specs=[SMEM] + [HBM] * 6,
        out_specs=(VMEM,) * 4,
        scratch_shapes=[
            pltpu.VMEM(cos_table.shape, jnp.float32),
            pltpu.VMEM(cos_table.shape, jnp.float32),
            pltpu.VMEM(tokens, jnp.bfloat16),
            pltpu.VMEM(tokens, jnp.bfloat16),
            pltpu.VMEM(tokens, jnp.bfloat16),
            pltpu.VMEM(tokens, jnp.bfloat16),
            pltpu.SemaphoreType.DMA((6,)),
        ],
        compiler_params=PARAMS,
        name="states",
    )(
        offsets,
        *(
            pltpu.with_memory_space_constraint(x, pltpu.HBM)
            for x in (jnp.asarray(cos_table), jnp.asarray(sin_table), queries, keys, values, out_grad)
        )
    )

    received = exchange(sent, "ctx", order)

    dq, dk, dv, part = pl.pallas_call(
        functools.partial(local_kernel, scale),
        out_shape=(shape(rows, width), shape(rows, width), shape(rows, width), shape(8, DIM)),
        in_specs=[VMEM] * 7,
        out_specs=(VMEM,) * 4,
        compiler_params=PARAMS,
        name="local_grads",
    )(gain_row, cosine, sine, queries, krot, values, out_grad)

    scanned = pl.pallas_call(
        functools.partial(scan_kernel, scale, shards),
        out_shape=shape(shards * BACK, DIM),
        in_specs=[VMEM] * 3,
        out_specs=VMEM,
        compiler_params=PARAMS,
        name="scan",
    )(gain_row, received, part)

    states = exchange(scanned, "ctx", order)

    gain_part = pl.pallas_call(
        functools.partial(gain_kernel, shards),
        out_shape=shape(groups * HEADS, DIM),
        in_specs=[VMEM],
        out_specs=VMEM,
        compiler_params=PARAMS,
        name="gain_part",
    )(states)
    gain_parts = exchange(gain_part, "dp", [(FIRST_DP + i) % groups for i in range(groups)])

    grad_queries, grad_keys, grad_values, grad_gain = pl.pallas_call(
        functools.partial(final_kernel, scale, factor),
        out_shape=(shape(*tokens, dtype=jnp.bfloat16),) * 3 + (shape(1, width),),
        in_specs=[VMEM] * 11,
        out_specs=(VMEM,) * 4,
        compiler_params=PARAMS,
        name="final",
    )(gain_row, cosine, sine, krot, values, out_grad, dq, dk, dv, states, gain_parts)
    return grad_queries, grad_keys, grad_values, grad_gain.reshape(width)


def solution(mesh):
    rows = P("dp", "ctx", None)
    return jax.shard_map(
        local,
        mesh=mesh,
        in_specs=(rows, rows, rows, rows, P(), P("dp", "ctx")),
        out_specs=(rows, rows, rows, P()),
        check_vma=False,
    )
```

```python
import functools

import jax
import jax.numpy as jnp
import numpy as np
from jax import lax
from jax.experimental import pallas as pl
from jax.experimental.pallas import tpu as pltpu
from jax.sharding import PartitionSpec as P

HEADS = 2
DIM = 128
HALF = 64
ROWS = 512
BASE = 500000.0
LOW, MIDDLE, HIGH = 32, 64, 65
TABLE = HIGH + MIDDLE + LOW
TABLE_ROWS = 168
SEND = 12
BACK = 10
CHUNKS = 2
SIDE = 8
FIRST = (4, 4)
FIRST_DP = 4


def rotary_tables():
    freqs = np.power(BASE, -2.0 * np.arange(HALF) / DIM).astype(np.float32).astype(np.float64)
    steps = np.concatenate([np.arange(HIGH) * 2048, np.arange(MIDDLE) * 32, np.arange(LOW)])
    angle = np.zeros((TABLE_ROWS, HALF))
    angle[:TABLE] = steps[:, None] * freqs[None, :]
    cosine, sine = np.cos(angle), np.sin(angle)
    return (
        np.concatenate([cosine, cosine], axis=1).astype(np.float32),
        np.concatenate([-sine, sine], axis=1).astype(np.float32),
    )


def dot(a, b, ca, cb):
    return lax.dot_general(a, b, (((ca,), (cb,)), ((), ())), preferred_element_type=jnp.float32)


def swap(x):
    return pltpu.roll(x, HALF, 1)


def states_kernel(
    off_ref, ctab_hbm, stab_hbm, q_hbm, k_hbm, v_hbm, g_hbm, send_ref, krot_ref, cos_ref, sin_ref,
    ctab_ref, stab_ref, q_ref, k_ref, v_ref, g_ref, sems,
):
    pairs = (
        (ctab_hbm, ctab_ref),
        (stab_hbm, stab_ref),
        (k_hbm, k_ref),
        (v_hbm, v_ref),
        (q_hbm, q_ref),
        (g_hbm, g_ref),
    )
    copies = [pltpu.make_async_copy(src, dst, sems.at[i]) for i, (src, dst) in enumerate(pairs)]
    for copy in copies:
        copy.start()
    for copy in copies[:2]:
        copy.wait()
    offset = off_ref[0, 0]
    high, middle, low = offset // 2048, (offset // 32) % 64, offset % 32

    def row(at):
        return ctab_ref[pl.ds(at, 1), :], stab_ref[pl.ds(at, 1), :]

    def add(left, right):
        (ca, sa), (cb, sb) = left, right
        return ca * cb - sa * sb, sa * cb + ca * sb

    start = add(add(row(high), row(HIGH + middle)), row(HIGH + MIDDLE + low))
    lows = (
        ctab_ref[HIGH + MIDDLE : HIGH + MIDDLE + LOW, :],
        stab_ref[HIGH + MIDDLE : HIGH + MIDDLE + LOW, :],
    )
    for block in range(ROWS // LOW):
        here = add(start, row(HIGH + block))
        cosine, sine = add(here, lows)
        cos_ref[block * LOW : (block + 1) * LOW, :] = cosine
        sin_ref[block * LOW : (block + 1) * LOW, :] = sine
    cosine, sine = cos_ref[...], sin_ref[...]
    for copy in copies[2:]:
        copy.wait()
    for head in range(HEADS):
        lanes = slice(head * DIM, (head + 1) * DIM)
        k = k_ref[0, :, lanes].astype(jnp.float32)
        krot = (k * cosine + swap(k) * sine).astype(jnp.bfloat16)
        krot_ref[:, lanes] = krot
        kv = dot(v_ref[0, :, lanes], krot, 0, 0)
        q = q_ref[0, :, lanes].astype(jnp.float32)
        pair = jnp.concatenate([q * cosine, q * -sine], axis=1).astype(jnp.bfloat16)
        gq = dot(g_ref[0, :, lanes], pair, 0, 0)
        for half in range(2):
            at = 2 * head + half
            rows = slice(half * HALF, (half + 1) * HALF)
            send_ref[pl.ds(at, HALF, stride=SEND), :] = kv[rows]
            send_ref[pl.ds(4 + at, HALF, stride=SEND), :] = gq[rows, :DIM]
            send_ref[pl.ds(8 + at, HALF, stride=SEND), :] = gq[rows, DIM:]


def local_kernel(
    scale, gain_ref, cos_ref, sin_ref, q_ref, krot_ref, v_ref, g_ref, dq_ref, dk_ref, dv_ref, part_ref
):
    cosine, sine = cos_ref[...], sin_ref[...]
    causal = lax.broadcasted_iota(jnp.int32, (ROWS, ROWS), 0) >= lax.broadcasted_iota(
        jnp.int32, (ROWS, ROWS), 1
    )
    part_ref[...] = jnp.zeros_like(part_ref)
    for head in range(HEADS):
        lanes = slice(head * DIM, (head + 1) * DIM)
        q = q_ref[0, :, lanes].astype(jnp.float32)
        scaled = q * gain_ref[:, lanes]
        qrot = (scaled * cosine + swap(scaled) * sine).astype(jnp.bfloat16)
        krot = krot_ref[:, lanes]
        v = v_ref[0, :, lanes]
        g = g_ref[0, :, lanes]
        attn = jnp.where(causal, scale * dot(qrot, krot, 1, 1), 0.0).astype(jnp.bfloat16)
        dattn = jnp.where(causal, scale * dot(g, v, 1, 1), 0.0).astype(jnp.bfloat16)
        dv_ref[:, lanes] = dot(attn, g, 0, 0)
        dk = dot(dattn, qrot, 0, 0)
        dk_ref[:, lanes] = dk * cosine - swap(dk) * sine
        dq = dot(dattn, krot, 1, 0)
        dq = dq * cosine - swap(dq) * sine
        dq_ref[:, lanes] = dq
        part_ref[head : head + 1, :] = jnp.sum(dq * q, axis=0, keepdims=True)


def rank(shard):
    return (shard // SIDE - FIRST[0]) % SIDE * SIDE + (shard % SIDE - FIRST[1]) % SIDE


def scan_kernel(scale, count, gain_ref, recv_ref, part_ref, send_ref):
    rows = lax.broadcasted_iota(jnp.int32, (8, DIM), 0)
    weight = jnp.where(rows % 4 < 2, gain_ref[:, :DIM], gain_ref[:, DIM:])

    before = jnp.zeros((8, DIM), jnp.float32)
    products = jnp.zeros((8, DIM), jnp.float32)
    for shard in range(count):
        source, target = SEND * rank(shard), BACK * rank(shard)
        twice = jnp.where(rows < 4, before, swap(pltpu.roll(before, 4, 0)))
        send_ref[target : target + 8, :] = twice
        products += twice * recv_ref[source + 4 : source + 12, :]
        before += recv_ref[source : source + 8, :]
    after = jnp.zeros((8, DIM), jnp.float32)
    for shard in reversed(range(count)):
        source, target = SEND * rank(shard), BACK * rank(shard)
        back = after * weight
        back = back + swap(pltpu.roll(back, 4, 0))
        send_ref[target + 4 : target + 8, :] = back[:4]
        after += recv_ref[source + 4 : source + 12, :]

    part = part_ref[...]
    for head in range(HEADS):
        mine = jnp.where(rows % 4 // 2 == head, products, 0.0)
        total = scale * jnp.sum(mine, axis=0, keepdims=True)
        part = part + jnp.where(rows == head, total, 0.0)
    for shard in range(count):
        send_ref[BACK * shard + 8 : BACK * shard + 10, :] = part[:HEADS]


def gain_kernel(count, recv_ref, out_ref):
    copies = out_ref.shape[0] // HEADS
    for head in range(HEADS):
        part = jnp.sum(recv_ref[pl.ds(8 + head, count, stride=BACK), :], axis=0, keepdims=True)
        for copy in range(copies):
            out_ref[HEADS * copy + head : HEADS * copy + head + 1, :] = part


def final_kernel(
    scale, factor, gain_ref, cos_ref, sin_ref, krot_ref, v_ref, g_ref, dq_ref, dk_ref, dv_ref, recv_ref, parts_ref,
    gq_hbm, gk_hbm, gv_hbm, total_hbm, gq_ref, gk_ref, gv_ref, total_ref, sems,
):
    copies = []

    def write(source, target):
        copies.append(pltpu.make_async_copy(source, target, sems.at[len(copies)]))
        copies[-1].start()

    states, backs = [], []
    for head in range(HEADS):
        lanes = slice(head * DIM, (head + 1) * DIM)
        parts = parts_ref[pl.ds(head, parts_ref.shape[0] // HEADS, stride=HEADS), :]
        total_ref[:, lanes] = jnp.sum(parts, axis=0, keepdims=True) * factor

        def matrix(first):
            halves = [recv_ref[pl.ds(first + half, HALF, stride=BACK), :] for half in range(2)]
            return scale * jnp.concatenate(halves, axis=0)

        states.append(matrix(2 * head))
        backs.append(matrix(4 + 2 * head))
    write(total_ref, total_hbm)

    def both(x):
        return jnp.concatenate([x, swap(x)], axis=1).astype(jnp.bfloat16)

    def unrotate(products, rows):
        return products[:, :DIM] * cos_ref[rows, :] - products[:, DIM:] * sin_ref[rows, :]

    states = [both(x) for x in states]
    backs = [both(x) for x in backs]
    for start in range(0, ROWS, ROWS // CHUNKS):
        rows = slice(start, start + ROWS // CHUNKS)
        for head in range(HEADS):
            lanes = slice(head * DIM, (head + 1) * DIM)
            dv = dot(krot_ref[rows, lanes], backs[head][:, :DIM], 1, 1)
            gv_ref[0, rows, lanes] = (dv_ref[rows, lanes] + dv).astype(jnp.bfloat16)
        write(gv_ref.at[:, rows], gv_hbm.at[:, rows])
        for head in range(HEADS):
            lanes = slice(head * DIM, (head + 1) * DIM)
            dq = dq_ref[rows, lanes] + unrotate(dot(g_ref[0, rows, lanes], states[head], 1, 0), rows)
            gq_ref[0, rows, lanes] = (dq * gain_ref[:, lanes]).astype(jnp.bfloat16)
        write(gq_ref.at[:, rows], gq_hbm.at[:, rows])
        for head in range(HEADS):
            lanes = slice(head * DIM, (head + 1) * DIM)
            dk = dk_ref[rows, lanes] + unrotate(dot(v_ref[0, rows, lanes], backs[head], 1, 0), rows)
            gk_ref[0, rows, lanes] = dk.astype(jnp.bfloat16)
        write(gk_ref.at[:, rows], gk_hbm.at[:, rows])
    for copy in copies:
        copy.wait()


VMEM = pl.BlockSpec(memory_space=pltpu.VMEM)
SMEM = pl.BlockSpec(memory_space=pltpu.SMEM)
HBM = pl.BlockSpec(memory_space=pltpu.HBM)
PARAMS = pltpu.CompilerParams(vmem_limit_bytes=24 * 1024 * 1024)


def shape(*dims, dtype=jnp.float32):
    return jax.ShapeDtypeStruct(dims, dtype)


def exchange(rows, axis, order=None):
    count = lax.axis_size(axis)
    pieces = rows.reshape(count, 1, rows.size // count)
    groups = None if order is None else [order]
    return lax.all_to_all(pieces, axis, 0, 0, axis_index_groups=groups, tiled=True).reshape(rows.shape)


def local(queries, keys, values, out_grad, q_gain, offsets):
    rows, width = queries.shape[1], queries.shape[2]
    shards, groups = lax.axis_size("ctx"), lax.axis_size("dp")
    scale = float((DIM * rows * shards) ** (-0.5))
    factor = float((rows * shards * groups) ** (-0.5))
    cos_table, sin_table = rotary_tables()
    gain_row = q_gain.reshape(1, width)
    order = sorted(range(shards), key=rank)
    tokens = queries.shape

    sent, krot, cosine, sine = pl.pallas_call(
        states_kernel,
        out_shape=(
            shape(shards * SEND, DIM),
            shape(rows, width, dtype=jnp.bfloat16),
            shape(rows, DIM),
            shape(rows, DIM),
        ),
        in_specs=[SMEM] + [HBM] * 6,
        out_specs=(VMEM,) * 4,
        scratch_shapes=[
            pltpu.VMEM(cos_table.shape, jnp.float32),
            pltpu.VMEM(cos_table.shape, jnp.float32),
            pltpu.VMEM(tokens, jnp.bfloat16),
            pltpu.VMEM(tokens, jnp.bfloat16),
            pltpu.VMEM(tokens, jnp.bfloat16),
            pltpu.VMEM(tokens, jnp.bfloat16),
            pltpu.SemaphoreType.DMA((6,)),
        ],
        compiler_params=PARAMS,
        name="states",
    )(
        offsets,
        *(
            pltpu.with_memory_space_constraint(x, pltpu.HBM)
            for x in (jnp.asarray(cos_table), jnp.asarray(sin_table), queries, keys, values, out_grad)
        )
    )

    received = exchange(sent, "ctx", order)

    dq, dk, dv, part = pl.pallas_call(
        functools.partial(local_kernel, scale),
        out_shape=(shape(rows, width), shape(rows, width), shape(rows, width), shape(8, DIM)),
        in_specs=[VMEM] * 7,
        out_specs=(VMEM,) * 4,
        compiler_params=PARAMS,
        name="local_grads",
    )(gain_row, cosine, sine, queries, krot, values, out_grad)

    scanned = pl.pallas_call(
        functools.partial(scan_kernel, scale, shards),
        out_shape=shape(shards * BACK, DIM),
        in_specs=[VMEM] * 3,
        out_specs=VMEM,
        compiler_params=PARAMS,
        name="scan",
    )(gain_row, received, part)

    states = exchange(scanned, "ctx", order)

    gain_part = pl.pallas_call(
        functools.partial(gain_kernel, shards),
        out_shape=shape(groups * HEADS, DIM),
        in_specs=[VMEM],
        out_specs=VMEM,
        compiler_params=PARAMS,
        name="gain_part",
    )(states)
    gain_parts = exchange(gain_part, "dp", [(FIRST_DP + i) % groups for i in range(groups)])

    grad_queries, grad_keys, grad_values, grad_gain = pl.pallas_call(
        functools.partial(final_kernel, scale, factor),
        out_shape=(shape(*tokens, dtype=jnp.bfloat16),) * 3 + (shape(1, width),),
        in_specs=[VMEM] * 11,
        out_specs=(HBM,) * 4,
        scratch_shapes=[
            pltpu.VMEM(tokens, jnp.bfloat16),
            pltpu.VMEM(tokens, jnp.bfloat16),
            pltpu.VMEM(tokens, jnp.bfloat16),
            pltpu.VMEM((1, width), jnp.float32),
            pltpu.SemaphoreType.DMA((1 + 3 * CHUNKS,)),
        ],
        compiler_params=PARAMS,
        name="final",
    )(gain_row, cosine, sine, krot, values, out_grad, dq, dk, dv, states, gain_parts)
    return grad_queries, grad_keys, grad_values, grad_gain.reshape(width)


def solution(mesh):
    rows = P("dp", "ctx", None)
    return jax.shard_map(
        local,
        mesh=mesh,
        in_specs=(rows, rows, rows, rows, P(), P("dp", "ctx")),
        out_specs=(rows, rows, rows, P()),
        check_vma=False,
    )
```

```python
import functools

import jax
import jax.numpy as jnp
import numpy as np
from jax import lax
from jax.experimental import pallas as pl
from jax.experimental.pallas import tpu as pltpu
from jax.sharding import PartitionSpec as P

HEADS = 2
DIM = 128
HALF = 64
ROWS = 512
BASE = 500000.0
LOW, MIDDLE, HIGH = 32, 64, 65
TABLE = HIGH + MIDDLE + LOW
TABLE_ROWS = 168
SEND = 12
BACK = 10
CHUNKS = 2
SIDE = 8
FIRST = (4, 4)
FIRST_DP = 4


def rotary_tables():
    freqs = np.power(BASE, -2.0 * np.arange(HALF) / DIM).astype(np.float32).astype(np.float64)
    steps = np.concatenate([np.arange(HIGH) * 2048, np.arange(MIDDLE) * 32, np.arange(LOW)])
    angle = np.zeros((TABLE_ROWS, HALF))
    angle[:TABLE] = steps[:, None] * freqs[None, :]
    cosine, sine = np.cos(angle), np.sin(angle)
    return (
        np.concatenate([cosine, cosine], axis=1).astype(np.float32),
        np.concatenate([-sine, sine], axis=1).astype(np.float32),
    )


def dot(a, b, ca, cb):
    return lax.dot_general(a, b, (((ca,), (cb,)), ((), ())), preferred_element_type=jnp.float32)


def swap(x):
    return pltpu.roll(x, HALF, 1)


def local_here(early):
    return (lax.rem(lax.axis_index("dp"), 2) == 0) == early


def states_kernel(
    scale, off_ref, ctab_hbm, stab_hbm, q_hbm, k_hbm, v_hbm, g_hbm, gain_hbm,
    send_ref, krot_ref, cos_ref, sin_ref, dq_ref, dk_ref, dv_ref, part_ref,
    ctab_ref, stab_ref, q_ref, k_ref, v_ref, g_ref, gain_ref, sems,
):
    pairs = (
        (ctab_hbm, ctab_ref),
        (stab_hbm, stab_ref),
        (k_hbm, k_ref),
        (v_hbm, v_ref),
        (q_hbm, q_ref),
        (g_hbm, g_ref),
        (gain_hbm, gain_ref),
    )
    copies = [pltpu.make_async_copy(src, dst, sems.at[i]) for i, (src, dst) in enumerate(pairs)]
    for copy in copies:
        copy.start()
    for copy in copies[:2]:
        copy.wait()
    offset = off_ref[0, 0]
    high, middle, low = offset // 2048, (offset // 32) % 64, offset % 32

    def row(at):
        return ctab_ref[pl.ds(at, 1), :], stab_ref[pl.ds(at, 1), :]

    def add(left, right):
        (ca, sa), (cb, sb) = left, right
        return ca * cb - sa * sb, sa * cb + ca * sb

    start = add(add(row(high), row(HIGH + middle)), row(HIGH + MIDDLE + low))
    lows = (
        ctab_ref[HIGH + MIDDLE : HIGH + MIDDLE + LOW, :],
        stab_ref[HIGH + MIDDLE : HIGH + MIDDLE + LOW, :],
    )
    for block in range(ROWS // LOW):
        here = add(start, row(HIGH + block))
        cosine, sine = add(here, lows)
        cos_ref[block * LOW : (block + 1) * LOW, :] = cosine
        sin_ref[block * LOW : (block + 1) * LOW, :] = sine
    cosine, sine = cos_ref[...], sin_ref[...]
    for copy in copies[2:]:
        copy.wait()
    for head in range(HEADS):
        lanes = slice(head * DIM, (head + 1) * DIM)
        k = k_ref[0, :, lanes].astype(jnp.float32)
        krot = (k * cosine + swap(k) * sine).astype(jnp.bfloat16)
        krot_ref[:, lanes] = krot
        kv = dot(v_ref[0, :, lanes], krot, 0, 0)
        q = q_ref[0, :, lanes].astype(jnp.float32)
        pair = jnp.concatenate([q * cosine, q * -sine], axis=1).astype(jnp.bfloat16)
        gq = dot(g_ref[0, :, lanes], pair, 0, 0)
        for half in range(2):
            at = 2 * head + half
            rows = slice(half * HALF, (half + 1) * HALF)
            send_ref[pl.ds(at, HALF, stride=SEND), :] = kv[rows]
            send_ref[pl.ds(4 + at, HALF, stride=SEND), :] = gq[rows, :DIM]
            send_ref[pl.ds(8 + at, HALF, stride=SEND), :] = gq[rows, DIM:]

    @pl.when(local_here(True))
    def _():
        local_grads(
            scale, gain_ref, cos_ref, sin_ref, q_ref, krot_ref, v_ref, g_ref, dq_ref, dk_ref, dv_ref, part_ref
        )


def local_grads(
    scale, gain_ref, cos_ref, sin_ref, q_ref, krot_ref, v_ref, g_ref, dq_ref, dk_ref, dv_ref, part_ref
):
    cosine, sine = cos_ref[...], sin_ref[...]
    causal = lax.broadcasted_iota(jnp.int32, (ROWS, ROWS), 0) >= lax.broadcasted_iota(
        jnp.int32, (ROWS, ROWS), 1
    )
    part_ref[...] = jnp.zeros_like(part_ref)
    for head in range(HEADS):
        lanes = slice(head * DIM, (head + 1) * DIM)
        q = q_ref[0, :, lanes].astype(jnp.float32)
        scaled = q * gain_ref[:, lanes]
        qrot = (scaled * cosine + swap(scaled) * sine).astype(jnp.bfloat16)
        krot = krot_ref[:, lanes]
        v = v_ref[0, :, lanes]
        g = g_ref[0, :, lanes]
        attn = jnp.where(causal, scale * dot(qrot, krot, 1, 1), 0.0).astype(jnp.bfloat16)
        dattn = jnp.where(causal, scale * dot(g, v, 1, 1), 0.0).astype(jnp.bfloat16)
        dv_ref[:, lanes] = dot(attn, g, 0, 0)
        dk = dot(dattn, qrot, 0, 0)
        dk_ref[:, lanes] = dk * cosine - swap(dk) * sine
        dq = dot(dattn, krot, 1, 0)
        dq = dq * cosine - swap(dq) * sine
        dq_ref[:, lanes] = dq
        part_ref[head : head + 1, :] = jnp.sum(dq * q, axis=0, keepdims=True)


def local_kernel(
    scale, gain_ref, cos_ref, sin_ref, q_ref, krot_ref, v_ref, g_ref, dq_in, dk_in, dv_in, part_in,
    dq_ref, dk_ref, dv_ref, part_ref,
):
    @pl.when(local_here(False))
    def _():
        local_grads(
            scale, gain_ref, cos_ref, sin_ref, q_ref, krot_ref, v_ref, g_ref, dq_ref, dk_ref, dv_ref, part_ref
        )

    @pl.when(local_here(True))
    def _():
        dq_ref[...] = dq_in[...]
        dk_ref[...] = dk_in[...]
        dv_ref[...] = dv_in[...]
        part_ref[...] = part_in[...]


def rank(shard):
    return (shard // SIDE - FIRST[0]) % SIDE * SIDE + (shard % SIDE - FIRST[1]) % SIDE


def scan_kernel(scale, count, gain_ref, recv_ref, part_ref, send_ref):
    rows = lax.broadcasted_iota(jnp.int32, (8, DIM), 0)
    weight = jnp.where(rows % 4 < 2, gain_ref[:, :DIM], gain_ref[:, DIM:])

    before = jnp.zeros((8, DIM), jnp.float32)
    products = jnp.zeros((8, DIM), jnp.float32)
    for shard in range(count):
        source, target = SEND * rank(shard), BACK * rank(shard)
        twice = jnp.where(rows < 4, before, swap(pltpu.roll(before, 4, 0)))
        send_ref[target : target + 8, :] = twice
        products += twice * recv_ref[source + 4 : source + 12, :]
        before += recv_ref[source : source + 8, :]
    after = jnp.zeros((8, DIM), jnp.float32)
    for shard in reversed(range(count)):
        source, target = SEND * rank(shard), BACK * rank(shard)
        back = after * weight
        back = back + swap(pltpu.roll(back, 4, 0))
        send_ref[target + 4 : target + 8, :] = back[:4]
        after += recv_ref[source + 4 : source + 12, :]

    part = part_ref[...]
    for head in range(HEADS):
        mine = jnp.where(rows % 4 // 2 == head, products, 0.0)
        total = scale * jnp.sum(mine, axis=0, keepdims=True)
        part = part + jnp.where(rows == head, total, 0.0)
    for shard in range(count):
        send_ref[BACK * shard + 8 : BACK * shard + 10, :] = part[:HEADS]


def gain_kernel(count, recv_ref, out_ref):
    copies = out_ref.shape[0] // HEADS
    for head in range(HEADS):
        part = jnp.sum(recv_ref[pl.ds(8 + head, count, stride=BACK), :], axis=0, keepdims=True)
        for copy in range(copies):
            out_ref[HEADS * copy + head : HEADS * copy + head + 1, :] = part


def final_kernel(
    scale, factor, gain_ref, cos_ref, sin_ref, krot_ref, v_ref, g_ref, dq_ref, dk_ref, dv_ref, recv_ref, parts_ref,
    gq_hbm, gk_hbm, gv_hbm, total_hbm, gq_ref, gk_ref, gv_ref, total_ref, sems,
):
    copies = []

    def write(source, target):
        copies.append(pltpu.make_async_copy(source, target, sems.at[len(copies)]))
        copies[-1].start()

    states, backs = [], []
    for head in range(HEADS):
        lanes = slice(head * DIM, (head + 1) * DIM)
        parts = parts_ref[pl.ds(head, parts_ref.shape[0] // HEADS, stride=HEADS), :]
        total_ref[:, lanes] = jnp.sum(parts, axis=0, keepdims=True) * factor

        def matrix(first):
            halves = [recv_ref[pl.ds(first + half, HALF, stride=BACK), :] for half in range(2)]
            return scale * jnp.concatenate(halves, axis=0)

        states.append(matrix(2 * head))
        backs.append(matrix(4 + 2 * head))
    write(total_ref, total_hbm)

    def both(x):
        return jnp.concatenate([x, swap(x)], axis=1).astype(jnp.bfloat16)

    def unrotate(products, rows):
        return products[:, :DIM] * cos_ref[rows, :] - products[:, DIM:] * sin_ref[rows, :]

    states = [both(x) for x in states]
    backs = [both(x) for x in backs]
    for start in range(0, ROWS, ROWS // CHUNKS):
        rows = slice(start, start + ROWS // CHUNKS)
        for head in range(HEADS):
            lanes = slice(head * DIM, (head + 1) * DIM)
            dv = dot(krot_ref[rows, lanes], backs[head][:, :DIM], 1, 1)
            gv_ref[0, rows, lanes] = (dv_ref[rows, lanes] + dv).astype(jnp.bfloat16)
        write(gv_ref.at[:, rows], gv_hbm.at[:, rows])
        for head in range(HEADS):
            lanes = slice(head * DIM, (head + 1) * DIM)
            dq = dq_ref[rows, lanes] + unrotate(dot(g_ref[0, rows, lanes], states[head], 1, 0), rows)
            gq_ref[0, rows, lanes] = (dq * gain_ref[:, lanes]).astype(jnp.bfloat16)
        write(gq_ref.at[:, rows], gq_hbm.at[:, rows])
        for head in range(HEADS):
            lanes = slice(head * DIM, (head + 1) * DIM)
            dk = dk_ref[rows, lanes] + unrotate(dot(v_ref[0, rows, lanes], backs[head], 1, 0), rows)
            gk_ref[0, rows, lanes] = dk.astype(jnp.bfloat16)
        write(gk_ref.at[:, rows], gk_hbm.at[:, rows])
    for copy in copies:
        copy.wait()


VMEM = pl.BlockSpec(memory_space=pltpu.VMEM)
SMEM = pl.BlockSpec(memory_space=pltpu.SMEM)
HBM = pl.BlockSpec(memory_space=pltpu.HBM)
PARAMS = pltpu.CompilerParams(vmem_limit_bytes=24 * 1024 * 1024)


def shape(*dims, dtype=jnp.float32):
    return jax.ShapeDtypeStruct(dims, dtype)


def exchange(rows, axis, order=None):
    count = lax.axis_size(axis)
    pieces = rows.reshape(count, 1, rows.size // count)
    groups = None if order is None else [order]
    return lax.all_to_all(pieces, axis, 0, 0, axis_index_groups=groups, tiled=True).reshape(rows.shape)


def local(queries, keys, values, out_grad, q_gain, offsets):
    rows, width = queries.shape[1], queries.shape[2]
    shards, groups = lax.axis_size("ctx"), lax.axis_size("dp")
    scale = float((DIM * rows * shards) ** (-0.5))
    factor = float((rows * shards * groups) ** (-0.5))
    cos_table, sin_table = rotary_tables()
    gain_row = q_gain.reshape(1, width)
    order = sorted(range(shards), key=rank)
    tokens = queries.shape

    local_shapes = (shape(rows, width),) * 3 + (shape(8, DIM),)
    sent, krot, cosine, sine, *early = pl.pallas_call(
        functools.partial(states_kernel, scale),
        out_shape=(
            shape(shards * SEND, DIM),
            shape(rows, width, dtype=jnp.bfloat16),
            shape(rows, DIM),
            shape(rows, DIM),
            *local_shapes,
        ),
        in_specs=[SMEM] + [HBM] * 7,
        out_specs=(VMEM,) * 8,
        scratch_shapes=[
            pltpu.VMEM(cos_table.shape, jnp.float32),
            pltpu.VMEM(cos_table.shape, jnp.float32),
            pltpu.VMEM(tokens, jnp.bfloat16),
            pltpu.VMEM(tokens, jnp.bfloat16),
            pltpu.VMEM(tokens, jnp.bfloat16),
            pltpu.VMEM(tokens, jnp.bfloat16),
            pltpu.VMEM((1, width), jnp.float32),
            pltpu.SemaphoreType.DMA((7,)),
        ],
        compiler_params=PARAMS,
        name="states",
    )(
        offsets,
        *(
            pltpu.with_memory_space_constraint(x, pltpu.HBM)
            for x in (
                jnp.asarray(cos_table), jnp.asarray(sin_table), queries, keys, values, out_grad, gain_row
            )
        ),
    )

    received = exchange(sent, "ctx", order)

    dq, dk, dv, part = pl.pallas_call(
        functools.partial(local_kernel, scale),
        out_shape=local_shapes,
        in_specs=[VMEM] * 11,
        out_specs=(VMEM,) * 4,
        input_output_aliases={7: 0, 8: 1, 9: 2, 10: 3},
        compiler_params=PARAMS,
        name="local_grads",
    )(gain_row, cosine, sine, queries, krot, values, out_grad, *early)

    scanned = pl.pallas_call(
        functools.partial(scan_kernel, scale, shards),
        out_shape=shape(shards * BACK, DIM),
        in_specs=[VMEM] * 3,
        out_specs=VMEM,
        compiler_params=PARAMS,
        name="scan",
    )(gain_row, received, part)

    states = exchange(scanned, "ctx", order)

    gain_part = pl.pallas_call(
        functools.partial(gain_kernel, shards),
        out_shape=shape(groups * HEADS, DIM),
        in_specs=[VMEM],
        out_specs=VMEM,
        compiler_params=PARAMS,
        name="gain_part",
    )(states)
    gain_parts = exchange(gain_part, "dp", [(FIRST_DP + i) % groups for i in range(groups)])

    grad_queries, grad_keys, grad_values, grad_gain = pl.pallas_call(
        functools.partial(final_kernel, scale, factor),
        out_shape=(shape(*tokens, dtype=jnp.bfloat16),) * 3 + (shape(1, width),),
        in_specs=[VMEM] * 11,
        out_specs=(HBM,) * 4,
        scratch_shapes=[
            pltpu.VMEM(tokens, jnp.bfloat16),
            pltpu.VMEM(tokens, jnp.bfloat16),
            pltpu.VMEM(tokens, jnp.bfloat16),
            pltpu.VMEM((1, width), jnp.float32),
            pltpu.SemaphoreType.DMA((1 + 3 * CHUNKS,)),
        ],
        compiler_params=PARAMS,
        name="final",
    )(gain_row, cosine, sine, krot, values, out_grad, dq, dk, dv, states, gain_parts)
    return grad_queries, grad_keys, grad_values, grad_gain.reshape(width)


def solution(mesh):
    rows = P("dp", "ctx", None)
    return jax.shard_map(
        local,
        mesh=mesh,
        in_specs=(rows, rows, rows, rows, P(), P("dp", "ctx")),
        out_specs=(rows, rows, rows, P()),
        check_vma=False,
    )
```

```python
import functools

import jax
import jax.numpy as jnp
import numpy as np
from jax import lax
from jax.experimental import pallas as pl
from jax.experimental.pallas import tpu as pltpu
from jax.sharding import PartitionSpec as P

HEADS = 2
DIM = 128
HALF = 64
ROWS = 512
BASE = 500000.0
LOW, MIDDLE, HIGH = 32, 64, 65
TABLE = HIGH + MIDDLE + LOW
TABLE_ROWS = 168
SEND = 12
BACK = 10
CHUNKS = 2
SIDE = 8
FIRST = (4, 4)
FIRST_DP = 5


def rotary_tables():
    freqs = np.power(BASE, -2.0 * np.arange(HALF) / DIM).astype(np.float32).astype(np.float64)
    steps = np.concatenate([np.arange(HIGH) * 2048, np.arange(MIDDLE) * 32, np.arange(LOW)])
    angle = np.zeros((TABLE_ROWS, HALF))
    angle[:TABLE] = steps[:, None] * freqs[None, :]
    cosine, sine = np.cos(angle), np.sin(angle)
    return (
        np.concatenate([cosine, cosine], axis=1).astype(np.float32),
        np.concatenate([-sine, sine], axis=1).astype(np.float32),
    )


def dot(a, b, ca, cb):
    return lax.dot_general(a, b, (((ca,), (cb,)), ((), ())), preferred_element_type=jnp.float32)


def swap(x):
    return pltpu.roll(x, HALF, 1)


def local_here(early):
    return (lax.rem(lax.axis_index("dp"), 2) == 0) == early


def states_kernel(
    scale, off_ref, ctab_hbm, stab_hbm, q_hbm, k_hbm, v_hbm, g_hbm, gain_hbm,
    send_ref, krot_ref, cos_ref, sin_ref, dq_ref, dk_ref, dv_ref, part_ref,
    ctab_ref, stab_ref, q_ref, k_ref, v_ref, g_ref, gain_ref, sems,
):
    pairs = (
        (ctab_hbm, ctab_ref),
        (stab_hbm, stab_ref),
        (k_hbm, k_ref),
        (v_hbm, v_ref),
        (q_hbm, q_ref),
        (g_hbm, g_ref),
        (gain_hbm, gain_ref),
    )
    copies = [pltpu.make_async_copy(src, dst, sems.at[i]) for i, (src, dst) in enumerate(pairs)]
    for copy in copies:
        copy.start()
    for copy in copies[:2]:
        copy.wait()
    offset = off_ref[0, 0]
    high, middle, low = offset // 2048, (offset // 32) % 64, offset % 32

    def row(at):
        return ctab_ref[pl.ds(at, 1), :], stab_ref[pl.ds(at, 1), :]

    def add(left, right):
        (ca, sa), (cb, sb) = left, right
        return ca * cb - sa * sb, sa * cb + ca * sb

    start = add(add(row(high), row(HIGH + middle)), row(HIGH + MIDDLE + low))
    lows = (
        ctab_ref[HIGH + MIDDLE : HIGH + MIDDLE + LOW, :],
        stab_ref[HIGH + MIDDLE : HIGH + MIDDLE + LOW, :],
    )
    for block in range(ROWS // LOW):
        here = add(start, row(HIGH + block))
        cosine, sine = add(here, lows)
        cos_ref[block * LOW : (block + 1) * LOW, :] = cosine
        sin_ref[block * LOW : (block + 1) * LOW, :] = sine
    cosine, sine = cos_ref[...], sin_ref[...]
    for copy in copies[2:]:
        copy.wait()
    for head in range(HEADS):
        lanes = slice(head * DIM, (head + 1) * DIM)
        k = k_ref[0, :, lanes].astype(jnp.float32)
        krot = (k * cosine + swap(k) * sine).astype(jnp.bfloat16)
        krot_ref[:, lanes] = krot
        kv = dot(v_ref[0, :, lanes], krot, 0, 0)
        q = q_ref[0, :, lanes].astype(jnp.float32)
        pair = jnp.concatenate([q * cosine, q * -sine], axis=1).astype(jnp.bfloat16)
        gq = dot(g_ref[0, :, lanes], pair, 0, 0)
        for half in range(2):
            at = 2 * head + half
            rows = slice(half * HALF, (half + 1) * HALF)
            send_ref[pl.ds(at, HALF, stride=SEND), :] = kv[rows]
            send_ref[pl.ds(4 + at, HALF, stride=SEND), :] = gq[rows, :DIM]
            send_ref[pl.ds(8 + at, HALF, stride=SEND), :] = gq[rows, DIM:]

    @pl.when(local_here(True))
    def _():
        local_grads(
            scale, gain_ref, cos_ref, sin_ref, q_ref, krot_ref, v_ref, g_ref, dq_ref, dk_ref, dv_ref, part_ref
        )


def local_grads(
    scale, gain_ref, cos_ref, sin_ref, q_ref, krot_ref, v_ref, g_ref, dq_ref, dk_ref, dv_ref, part_ref
):
    cosine, sine = cos_ref[...], sin_ref[...]
    causal = lax.broadcasted_iota(jnp.int32, (ROWS, ROWS), 0) >= lax.broadcasted_iota(
        jnp.int32, (ROWS, ROWS), 1
    )
    part_ref[...] = jnp.zeros_like(part_ref)
    for head in range(HEADS):
        lanes = slice(head * DIM, (head + 1) * DIM)
        q = q_ref[0, :, lanes].astype(jnp.float32)
        scaled = q * gain_ref[:, lanes]
        qrot = (scaled * cosine + swap(scaled) * sine).astype(jnp.bfloat16)
        krot = krot_ref[:, lanes]
        v = v_ref[0, :, lanes]
        g = g_ref[0, :, lanes]
        attn = jnp.where(causal, scale * dot(qrot, krot, 1, 1), 0.0).astype(jnp.bfloat16)
        dattn = jnp.where(causal, scale * dot(g, v, 1, 1), 0.0).astype(jnp.bfloat16)
        dv_ref[:, lanes] = dot(attn, g, 0, 0)
        dk = dot(dattn, qrot, 0, 0)
        dk_ref[:, lanes] = dk * cosine - swap(dk) * sine
        dq = dot(dattn, krot, 1, 0)
        dq = dq * cosine - swap(dq) * sine
        dq_ref[:, lanes] = dq
        part_ref[head : head + 1, :] = jnp.sum(dq * q, axis=0, keepdims=True)


def local_kernel(
    scale, gain_ref, cos_ref, sin_ref, q_ref, krot_ref, v_ref, g_ref, dq_in, dk_in, dv_in, part_in,
    dq_ref, dk_ref, dv_ref, part_ref,
):
    @pl.when(local_here(False))
    def _():
        local_grads(
            scale, gain_ref, cos_ref, sin_ref, q_ref, krot_ref, v_ref, g_ref, dq_ref, dk_ref, dv_ref, part_ref
        )

    @pl.when(local_here(True))
    def _():
        dq_ref[...] = dq_in[...]
        dk_ref[...] = dk_in[...]
        dv_ref[...] = dv_in[...]
        part_ref[...] = part_in[...]


def rank(shard):
    return (shard // SIDE - FIRST[0]) % SIDE * SIDE + (shard % SIDE - FIRST[1]) % SIDE


def scan_kernel(scale, count, gain_ref, recv_ref, part_ref, send_ref):
    rows = lax.broadcasted_iota(jnp.int32, (8, DIM), 0)
    weight = jnp.where(rows % 4 < 2, gain_ref[:, :DIM], gain_ref[:, DIM:])

    before = jnp.zeros((8, DIM), jnp.float32)
    products = jnp.zeros((8, DIM), jnp.float32)
    for shard in range(count):
        source, target = SEND * rank(shard), BACK * rank(shard)
        twice = jnp.where(rows < 4, before, swap(pltpu.roll(before, 4, 0)))
        send_ref[target : target + 8, :] = twice
        products += twice * recv_ref[source + 4 : source + 12, :]
        before += recv_ref[source : source + 8, :]
    after = jnp.zeros((8, DIM), jnp.float32)
    for shard in reversed(range(count)):
        source, target = SEND * rank(shard), BACK * rank(shard)
        back = after * weight
        back = back + swap(pltpu.roll(back, 4, 0))
        send_ref[target + 4 : target + 8, :] = back[:4]
        after += recv_ref[source + 4 : source + 12, :]

    part = part_ref[...]
    for head in range(HEADS):
        mine = jnp.where(rows % 4 // 2 == head, products, 0.0)
        total = scale * jnp.sum(mine, axis=0, keepdims=True)
        part = part + jnp.where(rows == head, total, 0.0)
    for shard in range(count):
        send_ref[BACK * shard + 8 : BACK * shard + 10, :] = part[:HEADS]


def gain_kernel(count, recv_ref, out_ref):
    copies = out_ref.shape[0] // HEADS
    for head in range(HEADS):
        part = jnp.sum(recv_ref[pl.ds(8 + head, count, stride=BACK), :], axis=0, keepdims=True)
        for copy in range(copies):
            out_ref[HEADS * copy + head : HEADS * copy + head + 1, :] = part


def write_grads(
    scale, gain_ref, cos_ref, sin_ref, krot_ref, v_ref, g_ref, dq_ref, dk_ref, dv_ref, recv_ref,
    gq_hbm, gk_hbm, gv_hbm, gq_ref, gk_ref, gv_ref, sems,
):
    copies = []

    def write(source, target):
        copies.append(pltpu.make_async_copy(source, target, sems.at[len(copies)]))
        copies[-1].start()

    def matrix(first):
        halves = [recv_ref[pl.ds(first + half, HALF, stride=BACK), :] for half in range(2)]
        return scale * jnp.concatenate(halves, axis=0)

    def both(x):
        return jnp.concatenate([x, swap(x)], axis=1).astype(jnp.bfloat16)

    def unrotate(products, rows):
        return products[:, :DIM] * cos_ref[rows, :] - products[:, DIM:] * sin_ref[rows, :]

    states = [both(matrix(2 * head)) for head in range(HEADS)]
    backs = [both(matrix(4 + 2 * head)) for head in range(HEADS)]
    for start in range(0, ROWS, ROWS // CHUNKS):
        rows = slice(start, start + ROWS // CHUNKS)
        for head in range(HEADS):
            lanes = slice(head * DIM, (head + 1) * DIM)
            dv = dot(krot_ref[rows, lanes], backs[head][:, :DIM], 1, 1)
            gv_ref[0, rows, lanes] = (dv_ref[rows, lanes] + dv).astype(jnp.bfloat16)
        write(gv_ref.at[:, rows], gv_hbm.at[:, rows])
        for head in range(HEADS):
            lanes = slice(head * DIM, (head + 1) * DIM)
            dq = dq_ref[rows, lanes] + unrotate(dot(g_ref[0, rows, lanes], states[head], 1, 0), rows)
            gq_ref[0, rows, lanes] = (dq * gain_ref[:, lanes]).astype(jnp.bfloat16)
        write(gq_ref.at[:, rows], gq_hbm.at[:, rows])
        for head in range(HEADS):
            lanes = slice(head * DIM, (head + 1) * DIM)
            dk = dk_ref[rows, lanes] + unrotate(dot(v_ref[0, rows, lanes], backs[head], 1, 0), rows)
            gk_ref[0, rows, lanes] = dk.astype(jnp.bfloat16)
        write(gk_ref.at[:, rows], gk_hbm.at[:, rows])
    for copy in copies:
        copy.wait()


def waiting_kernel(scale, *refs):
    @pl.when(local_here(False))
    def _():
        write_grads(scale, *refs)


def final_kernel(scale, factor, *refs):
    operands, parts_ref, grads, total_hbm = refs[:10], refs[10], refs[14:17], refs[17]
    *scratch, sems, total_ref, total_sem = refs[18:]
    for head in range(HEADS):
        lanes = slice(head * DIM, (head + 1) * DIM)
        parts = parts_ref[pl.ds(head, parts_ref.shape[0] // HEADS, stride=HEADS), :]
        total_ref[:, lanes] = jnp.sum(parts, axis=0, keepdims=True) * factor
    copy = pltpu.make_async_copy(total_ref, total_hbm, total_sem)
    copy.start()

    @pl.when(local_here(True))
    def _():
        write_grads(scale, *operands, *grads, *scratch, sems)

    copy.wait()


VMEM = pl.BlockSpec(memory_space=pltpu.VMEM)
SMEM = pl.BlockSpec(memory_space=pltpu.SMEM)
HBM = pl.BlockSpec(memory_space=pltpu.HBM)
PARAMS = pltpu.CompilerParams(vmem_limit_bytes=24 * 1024 * 1024)


def shape(*dims, dtype=jnp.float32):
    return jax.ShapeDtypeStruct(dims, dtype)


def exchange(rows, axis, order=None):
    count = lax.axis_size(axis)
    pieces = rows.reshape(count, 1, rows.size // count)
    groups = None if order is None else [order]
    return lax.all_to_all(pieces, axis, 0, 0, axis_index_groups=groups, tiled=True).reshape(rows.shape)


def local(queries, keys, values, out_grad, q_gain, offsets):
    rows, width = queries.shape[1], queries.shape[2]
    shards, groups = lax.axis_size("ctx"), lax.axis_size("dp")
    scale = float((DIM * rows * shards) ** (-0.5))
    factor = float((rows * shards * groups) ** (-0.5))
    cos_table, sin_table = rotary_tables()
    gain_row = q_gain.reshape(1, width)
    order = sorted(range(shards), key=rank)
    tokens = queries.shape

    local_shapes = (shape(rows, width),) * 3 + (shape(8, DIM),)
    sent, krot, cosine, sine, *early = pl.pallas_call(
        functools.partial(states_kernel, scale),
        out_shape=(
            shape(shards * SEND, DIM),
            shape(rows, width, dtype=jnp.bfloat16),
            shape(rows, DIM),
            shape(rows, DIM),
            *local_shapes,
        ),
        in_specs=[SMEM] + [HBM] * 7,
        out_specs=(VMEM,) * 8,
        scratch_shapes=[
            pltpu.VMEM(cos_table.shape, jnp.float32),
            pltpu.VMEM(cos_table.shape, jnp.float32),
            pltpu.VMEM(tokens, jnp.bfloat16),
            pltpu.VMEM(tokens, jnp.bfloat16),
            pltpu.VMEM(tokens, jnp.bfloat16),
            pltpu.VMEM(tokens, jnp.bfloat16),
            pltpu.VMEM((1, width), jnp.float32),
            pltpu.SemaphoreType.DMA((7,)),
        ],
        compiler_params=PARAMS,
        name="states",
    )(
        offsets,
        *(
            pltpu.with_memory_space_constraint(x, pltpu.HBM)
            for x in (
                jnp.asarray(cos_table), jnp.asarray(sin_table), queries, keys, values, out_grad, gain_row
            )
        ),
    )

    received = exchange(sent, "ctx", order)

    dq, dk, dv, part = pl.pallas_call(
        functools.partial(local_kernel, scale),
        out_shape=local_shapes,
        in_specs=[VMEM] * 11,
        out_specs=(VMEM,) * 4,
        input_output_aliases={7: 0, 8: 1, 9: 2, 10: 3},
        compiler_params=PARAMS,
        name="local_grads",
    )(gain_row, cosine, sine, queries, krot, values, out_grad, *early)

    scanned = pl.pallas_call(
        functools.partial(scan_kernel, scale, shards),
        out_shape=shape(shards * BACK, DIM),
        in_specs=[VMEM] * 3,
        out_specs=VMEM,
        compiler_params=PARAMS,
        name="scan",
    )(gain_row, received, part)

    states = exchange(scanned, "ctx", order)

    gain_part = pl.pallas_call(
        functools.partial(gain_kernel, shards),
        out_shape=shape(groups * HEADS, DIM),
        in_specs=[VMEM],
        out_specs=VMEM,
        compiler_params=PARAMS,
        name="gain_part",
    )(states)

    operands = (gain_row, cosine, sine, krot, values, out_grad, dq, dk, dv, states)
    grad_shapes = (shape(*tokens, dtype=jnp.bfloat16),) * 3
    scratch = [pltpu.VMEM(tokens, jnp.bfloat16)] * 3 + [pltpu.SemaphoreType.DMA((3 * CHUNKS,))]
    grads = pl.pallas_call(
        functools.partial(waiting_kernel, scale),
        out_shape=grad_shapes,
        in_specs=[VMEM] * 10,
        out_specs=(HBM,) * 3,
        scratch_shapes=scratch,
        compiler_params=PARAMS,
        name="final_core1",
    )(*operands)

    gain_part, grads = lax.optimization_barrier((gain_part, grads))
    gain_parts = exchange(gain_part, "dp", [(FIRST_DP + i) % groups for i in range(groups)])

    grad_queries, grad_keys, grad_values, grad_gain = pl.pallas_call(
        functools.partial(final_kernel, scale, factor),
        out_shape=grad_shapes + (shape(1, width),),
        in_specs=[VMEM] * 11 + [HBM] * 3,
        out_specs=(HBM,) * 4,
        scratch_shapes=scratch + [pltpu.VMEM((1, width), jnp.float32), pltpu.SemaphoreType.DMA],
        input_output_aliases={11: 0, 12: 1, 13: 2},
        compiler_params=PARAMS,
        name="final",
    )(*operands, gain_parts, *grads)
    return grad_queries, grad_keys, grad_values, grad_gain.reshape(width)


def solution(mesh):
    rows = P("dp", "ctx", None)
    return jax.shard_map(
        local,
        mesh=mesh,
        in_specs=(rows, rows, rows, rows, P(), P("dp", "ctx")),
        out_specs=(rows, rows, rows, P()),
        check_vma=False,
    )
```

```python
import functools

import jax
import jax.numpy as jnp
import numpy as np
from jax import lax
from jax.experimental import pallas as pl
from jax.experimental.pallas import tpu as pltpu
from jax.sharding import PartitionSpec as P

HEADS = 2
DIM = 128
HALF = 64
ROWS = 512
BASE = 500000.0
LOW, MIDDLE, HIGH = 32, 64, 65
TABLE = HIGH + MIDDLE + LOW
TABLE_ROWS = 168
SEND = 12
BACK = 10
CHUNKS = 2
SIDE = 8
FIRST = (4, 4)
FIRST_DP = 5


def rotary_tables():
    freqs = np.power(BASE, -2.0 * np.arange(HALF) / DIM).astype(np.float32).astype(np.float64)
    steps = np.concatenate([np.arange(HIGH) * 2048, np.arange(MIDDLE) * 32, np.arange(LOW)])
    angle = np.zeros((TABLE_ROWS, HALF))
    angle[:TABLE] = steps[:, None] * freqs[None, :]
    cosine, sine = np.cos(angle), np.sin(angle)
    return (
        np.concatenate([cosine, cosine], axis=1).astype(np.float32),
        np.concatenate([-sine, sine], axis=1).astype(np.float32),
    )


def dot(a, b, ca, cb):
    return lax.dot_general(a, b, (((ca,), (cb,)), ((), ())), preferred_element_type=jnp.float32)


def swap(x):
    return pltpu.roll(x, HALF, 1)


def local_here(early):
    return (lax.rem(lax.axis_index("dp"), 2) == 0) == early


def states_kernel(
    scale, off_ref, ctab_hbm, stab_hbm, q_hbm, k_hbm, v_hbm, g_hbm, gain_hbm,
    send_ref, krot_ref, cos_ref, sin_ref, dq_ref, dk_ref, dv_ref, part_ref,
    ctab_ref, stab_ref, q_ref, k_ref, v_ref, g_ref, gain_ref, sems,
):
    pairs = (
        (ctab_hbm, ctab_ref),
        (stab_hbm, stab_ref),
        (k_hbm, k_ref),
        (v_hbm, v_ref),
        (q_hbm, q_ref),
        (g_hbm, g_ref),
        (gain_hbm, gain_ref),
    )
    copies = [pltpu.make_async_copy(src, dst, sems.at[i]) for i, (src, dst) in enumerate(pairs)]
    for copy in copies:
        copy.start()
    for copy in copies[:2]:
        copy.wait()
    offset = off_ref[0, 0]
    high, middle, low = offset // 2048, (offset // 32) % 64, offset % 32

    def row(at):
        return ctab_ref[pl.ds(at, 1), :], stab_ref[pl.ds(at, 1), :]

    def add(left, right):
        (ca, sa), (cb, sb) = left, right
        return ca * cb - sa * sb, sa * cb + ca * sb

    start = add(add(row(high), row(HIGH + middle)), row(HIGH + MIDDLE + low))
    lows = (
        ctab_ref[HIGH + MIDDLE : HIGH + MIDDLE + LOW, :],
        stab_ref[HIGH + MIDDLE : HIGH + MIDDLE + LOW, :],
    )
    for block in range(ROWS // LOW):
        here = add(start, row(HIGH + block))
        cosine, sine = add(here, lows)
        cos_ref[block * LOW : (block + 1) * LOW, :] = cosine
        sin_ref[block * LOW : (block + 1) * LOW, :] = sine
    cosine, sine = cos_ref[...], sin_ref[...]
    for copy in copies[2:]:
        copy.wait()
    for head in range(HEADS):
        lanes = slice(head * DIM, (head + 1) * DIM)
        k = k_ref[0, :, lanes].astype(jnp.float32)
        krot = (k * cosine + swap(k) * sine).astype(jnp.bfloat16)
        krot_ref[:, lanes] = krot
        kv = dot(v_ref[0, :, lanes], krot, 0, 0)
        q = q_ref[0, :, lanes].astype(jnp.float32)
        pair = jnp.concatenate([q * cosine, q * -sine], axis=1).astype(jnp.bfloat16)
        gq = dot(g_ref[0, :, lanes], pair, 0, 0)
        for half in range(2):
            at = 2 * head + half
            rows = slice(half * HALF, (half + 1) * HALF)
            send_ref[pl.ds(at, HALF, stride=SEND), :] = kv[rows]
            send_ref[pl.ds(4 + at, HALF, stride=SEND), :] = gq[rows, :DIM]
            send_ref[pl.ds(8 + at, HALF, stride=SEND), :] = gq[rows, DIM:]

    @pl.when(local_here(True))
    def _():
        local_grads(
            scale, gain_ref, cos_ref, sin_ref, q_ref, krot_ref, v_ref, g_ref, dq_ref, dk_ref, dv_ref, part_ref
        )


def local_grads(
    scale, gain_ref, cos_ref, sin_ref, q_ref, krot_ref, v_ref, g_ref, dq_ref, dk_ref, dv_ref, part_ref
):
    cosine, sine = cos_ref[...], sin_ref[...]
    causal = lax.broadcasted_iota(jnp.int32, (ROWS, ROWS), 0) >= lax.broadcasted_iota(
        jnp.int32, (ROWS, ROWS), 1
    )
    part_ref[...] = jnp.zeros_like(part_ref)
    for head in range(HEADS):
        lanes = slice(head * DIM, (head + 1) * DIM)
        q = q_ref[0, :, lanes].astype(jnp.float32)
        scaled = q * gain_ref[:, lanes]
        qrot = (scaled * cosine + swap(scaled) * sine).astype(jnp.bfloat16)
        krot = krot_ref[:, lanes]
        v = v_ref[0, :, lanes]
        g = g_ref[0, :, lanes]
        attn = jnp.where(causal, scale * dot(qrot, krot, 1, 1), 0.0).astype(jnp.bfloat16)
        dattn = jnp.where(causal, scale * dot(g, v, 1, 1), 0.0).astype(jnp.bfloat16)
        dv_ref[:, lanes] = dot(attn, g, 0, 0)
        dk = dot(dattn, qrot, 0, 0)
        dk_ref[:, lanes] = dk * cosine - swap(dk) * sine
        dq = dot(dattn, krot, 1, 0)
        dq = dq * cosine - swap(dq) * sine
        dq_ref[:, lanes] = dq
        part_ref[head : head + 1, :] = jnp.sum(dq * q, axis=0, keepdims=True)


def local_kernel(
    scale, gain_ref, cos_ref, sin_ref, q_ref, krot_ref, v_ref, g_ref, dq_in, dk_in, dv_in, part_in,
    dq_ref, dk_ref, dv_ref, part_ref,
):
    @pl.when(local_here(False))
    def _():
        local_grads(
            scale, gain_ref, cos_ref, sin_ref, q_ref, krot_ref, v_ref, g_ref, dq_ref, dk_ref, dv_ref, part_ref
        )

    @pl.when(local_here(True))
    def _():
        dq_ref[...] = dq_in[...]
        dk_ref[...] = dk_in[...]
        dv_ref[...] = dv_in[...]
        part_ref[...] = part_in[...]


def rank(shard):
    return (shard // SIDE - FIRST[0]) % SIDE * SIDE + (shard % SIDE - FIRST[1]) % SIDE


def scan_kernel(scale, count, gain_ref, recv_ref, part_ref, send_ref):
    rows = lax.broadcasted_iota(jnp.int32, (8, DIM), 0)
    weight = jnp.where(rows % 4 < 2, gain_ref[:, :DIM], gain_ref[:, DIM:])

    before = jnp.zeros((8, DIM), jnp.float32)
    products = jnp.zeros((8, DIM), jnp.float32)
    for shard in range(count):
        source, target = SEND * rank(shard), BACK * rank(shard)
        twice = jnp.where(rows < 4, before, swap(pltpu.roll(before, 4, 0)))
        send_ref[target : target + 8, :] = twice
        products += twice * recv_ref[source + 4 : source + 12, :]
        before += recv_ref[source : source + 8, :]
    after = jnp.zeros((8, DIM), jnp.float32)
    for shard in reversed(range(count)):
        source, target = SEND * rank(shard), BACK * rank(shard)
        back = after * weight
        back = back + swap(pltpu.roll(back, 4, 0))
        send_ref[target + 4 : target + 8, :] = back[:4]
        after += recv_ref[source + 4 : source + 12, :]

    part = part_ref[...]
    for head in range(HEADS):
        mine = jnp.where(rows % 4 // 2 == head, products, 0.0)
        total = scale * jnp.sum(mine, axis=0, keepdims=True)
        part = part + jnp.where(rows == head, total, 0.0)
    for shard in range(count):
        send_ref[BACK * shard + 8 : BACK * shard + 10, :] = part[:HEADS]


def gain_kernel(count, recv_ref, out_ref):
    copies = out_ref.shape[0] // HEADS
    for head in range(HEADS):
        part = jnp.sum(recv_ref[pl.ds(8 + head, count, stride=BACK), :], axis=0, keepdims=True)
        for copy in range(copies):
            out_ref[HEADS * copy + head : HEADS * copy + head + 1, :] = part


def write_grads(
    scale, gain_ref, cos_ref, sin_ref, krot_ref, v_ref, g_ref, dq_ref, dk_ref, dv_ref, recv_ref,
    gq_hbm, gk_hbm, gv_hbm, gq_ref, gk_ref, gv_ref, sems,
):
    copies = []

    def write(source, target):
        copies.append(pltpu.make_async_copy(source, target, sems.at[len(copies)]))
        copies[-1].start()

    def matrix(first):
        halves = [recv_ref[pl.ds(first + half, HALF, stride=BACK), :] for half in range(2)]
        return scale * jnp.concatenate(halves, axis=0)

    def both(x):
        return jnp.concatenate([x, swap(x)], axis=1).astype(jnp.bfloat16)

    def unrotate(products, rows):
        return products[:, :DIM] * cos_ref[rows, :] - products[:, DIM:] * sin_ref[rows, :]

    states = [both(matrix(2 * head)) for head in range(HEADS)]
    backs = [both(matrix(4 + 2 * head)) for head in range(HEADS)]
    for start in range(0, ROWS, ROWS // CHUNKS):
        rows = slice(start, start + ROWS // CHUNKS)
        for head in range(HEADS):
            lanes = slice(head * DIM, (head + 1) * DIM)
            dv = dot(krot_ref[rows, lanes], backs[head][:, :DIM], 1, 1)
            gv_ref[0, rows, lanes] = (dv_ref[rows, lanes] + dv).astype(jnp.bfloat16)
        write(gv_ref.at[:, rows], gv_hbm.at[:, rows])
        for head in range(HEADS):
            lanes = slice(head * DIM, (head + 1) * DIM)
            dq = dq_ref[rows, lanes] + unrotate(dot(g_ref[0, rows, lanes], states[head], 1, 0), rows)
            gq_ref[0, rows, lanes] = (dq * gain_ref[:, lanes]).astype(jnp.bfloat16)
        write(gq_ref.at[:, rows], gq_hbm.at[:, rows])
        for head in range(HEADS):
            lanes = slice(head * DIM, (head + 1) * DIM)
            dk = dk_ref[rows, lanes] + unrotate(dot(v_ref[0, rows, lanes], backs[head], 1, 0), rows)
            gk_ref[0, rows, lanes] = dk.astype(jnp.bfloat16)
        write(gk_ref.at[:, rows], gk_hbm.at[:, rows])
    for copy in copies:
        copy.wait()


def waiting_kernel(scale, count, *refs):
    gain_kernel(count, refs[9], refs[13])

    @pl.when(local_here(False))
    def _():
        write_grads(scale, *refs[:13], *refs[14:])


def final_kernel(scale, factor, *refs):
    operands, parts_ref, grads, total_hbm = refs[:10], refs[10], refs[14:17], refs[17]
    *scratch, sems, total_ref, total_sem = refs[18:]
    for head in range(HEADS):
        lanes = slice(head * DIM, (head + 1) * DIM)
        parts = parts_ref[pl.ds(head, parts_ref.shape[0] // HEADS, stride=HEADS), :]
        total_ref[:, lanes] = jnp.sum(parts, axis=0, keepdims=True) * factor
    copy = pltpu.make_async_copy(total_ref, total_hbm, total_sem)
    copy.start()

    @pl.when(local_here(True))
    def _():
        write_grads(scale, *operands, *grads, *scratch, sems)

    copy.wait()


VMEM = pl.BlockSpec(memory_space=pltpu.VMEM)
SMEM = pl.BlockSpec(memory_space=pltpu.SMEM)
HBM = pl.BlockSpec(memory_space=pltpu.HBM)
PARAMS = pltpu.CompilerParams(vmem_limit_bytes=24 * 1024 * 1024)


def shape(*dims, dtype=jnp.float32):
    return jax.ShapeDtypeStruct(dims, dtype)


def exchange(rows, axis, order=None):
    count = lax.axis_size(axis)
    pieces = rows.reshape(count, 1, rows.size // count)
    groups = None if order is None else [order]
    return lax.all_to_all(pieces, axis, 0, 0, axis_index_groups=groups, tiled=True).reshape(rows.shape)


def local(queries, keys, values, out_grad, q_gain, offsets):
    rows, width = queries.shape[1], queries.shape[2]
    shards, groups = lax.axis_size("ctx"), lax.axis_size("dp")
    scale = float((DIM * rows * shards) ** (-0.5))
    factor = float((rows * shards * groups) ** (-0.5))
    cos_table, sin_table = rotary_tables()
    gain_row = q_gain.reshape(1, width)
    order = sorted(range(shards), key=rank)
    tokens = queries.shape

    local_shapes = (shape(rows, width),) * 3 + (shape(8, DIM),)
    sent, krot, cosine, sine, *early = pl.pallas_call(
        functools.partial(states_kernel, scale),
        out_shape=(
            shape(shards * SEND, DIM),
            shape(rows, width, dtype=jnp.bfloat16),
            shape(rows, DIM),
            shape(rows, DIM),
            *local_shapes,
        ),
        in_specs=[SMEM] + [HBM] * 7,
        out_specs=(VMEM,) * 8,
        scratch_shapes=[
            pltpu.VMEM(cos_table.shape, jnp.float32),
            pltpu.VMEM(cos_table.shape, jnp.float32),
            pltpu.VMEM(tokens, jnp.bfloat16),
            pltpu.VMEM(tokens, jnp.bfloat16),
            pltpu.VMEM(tokens, jnp.bfloat16),
            pltpu.VMEM(tokens, jnp.bfloat16),
            pltpu.VMEM((1, width), jnp.float32),
            pltpu.SemaphoreType.DMA((7,)),
        ],
        compiler_params=PARAMS,
        name="states",
    )(
        offsets,
        *(
            pltpu.with_memory_space_constraint(x, pltpu.HBM)
            for x in (
                jnp.asarray(cos_table), jnp.asarray(sin_table), queries, keys, values, out_grad, gain_row
            )
        ),
    )

    received = exchange(sent, "ctx", order)

    dq, dk, dv, part = pl.pallas_call(
        functools.partial(local_kernel, scale),
        out_shape=local_shapes,
        in_specs=[VMEM] * 11,
        out_specs=(VMEM,) * 4,
        input_output_aliases={7: 0, 8: 1, 9: 2, 10: 3},
        compiler_params=PARAMS,
        name="local_grads",
    )(gain_row, cosine, sine, queries, krot, values, out_grad, *early)

    scanned = pl.pallas_call(
        functools.partial(scan_kernel, scale, shards),
        out_shape=shape(shards * BACK, DIM),
        in_specs=[VMEM] * 3,
        out_specs=VMEM,
        compiler_params=PARAMS,
        name="scan",
    )(gain_row, received, part)

    states = exchange(scanned, "ctx", order)

    operands = (gain_row, cosine, sine, krot, values, out_grad, dq, dk, dv, states)
    grad_shapes = (shape(*tokens, dtype=jnp.bfloat16),) * 3
    scratch = [pltpu.VMEM(tokens, jnp.bfloat16)] * 3 + [pltpu.SemaphoreType.DMA((3 * CHUNKS,))]
    *grads, gain_part = pl.pallas_call(
        functools.partial(waiting_kernel, scale, shards),
        out_shape=grad_shapes + (shape(groups * HEADS, DIM),),
        in_specs=[VMEM] * 10,
        out_specs=(HBM,) * 3 + (VMEM,),
        scratch_shapes=scratch,
        compiler_params=PARAMS,
        name="final_core1",
    )(*operands)

    gain_parts = exchange(gain_part, "dp", [(FIRST_DP + i) % groups for i in range(groups)])

    grad_queries, grad_keys, grad_values, grad_gain = pl.pallas_call(
        functools.partial(final_kernel, scale, factor),
        out_shape=grad_shapes + (shape(1, width),),
        in_specs=[VMEM] * 11 + [HBM] * 3,
        out_specs=(HBM,) * 4,
        scratch_shapes=scratch + [pltpu.VMEM((1, width), jnp.float32), pltpu.SemaphoreType.DMA],
        input_output_aliases={11: 0, 12: 1, 13: 2},
        compiler_params=PARAMS,
        name="final",
    )(*operands, gain_parts, *grads)
    return grad_queries, grad_keys, grad_values, grad_gain.reshape(width)


def solution(mesh):
    rows = P("dp", "ctx", None)
    return jax.shard_map(
        local,
        mesh=mesh,
        in_specs=(rows, rows, rows, rows, P(), P("dp", "ctx")),
        out_specs=(rows, rows, rows, P()),
        check_vma=False,
    )
```
